512 devices in a mesh: batch: 128 (over z, x, core), tower: 4 (over y).
Axes of the slice: x: 4, y: 4, z: 16, core: 2. Of those that a mesh axis runs over, the one named last changes fastest.
Arguments:
- images: bfloat16 [65536, 1152], P('batch'), may hold values from -13 to 13
- texts: bfloat16 [65536, 1152], P(('batch', 'tower')), may hold values from -13 to 13
- log_scale: float32 [], replicated, may hold values from 1.5 to 3
- bias: float32 [], replicated, may hold values from -2 to 0.5
- block_mask: int32 [256, 8], P('batch'), may hold values from 0 to 1, as said below
- data_order: int32 [65536], P(('batch', 'tower')), may hold values from 0 to 65535, as said below
Outputs:
- image_grad: float32 [65536, 1152], P(('batch', 'tower'))
- text_grad: float32 [65536, 1152], P(('batch', 'tower'))
- pair_loss: float32 [], replicated
The draws below stay inside these ranges and needn't reach their ends.
Inputs may be any that keep to these rules, and one draw needn't show every extreme that they name: block_mask[p, c] refers to text block 2 * (p // 2) + c; it is 1 exactly where that block exists and belongs to the same cluster as block p, clusters being runs of consecutive blocks of uneven lengths; so it is 1 for c = p % 2 and 0 for blocks past the last. data_order is a permutation; data_order[i] // 128 % 4 equals i // 128 % 4; the 128 rows of each run i // 128 send exactly 1 row to each batch index b, meaning data_order // 512 == b.
All inputs are finite; a program needn't handle non-finite values.
Results may differ from the reference program's by a relative error of at most 0.00031.
Values may be sent and summed in bfloat16 or wider, within the bound.
A program may use at most 64 MiB of HBM per device.

```python
import jax
import jax.numpy as jnp
from jax import lax

D = 1152
BLOCK = 256
WINDOW = 4
BLK_GROUP = 2
QUARTER = 128
TOKENS = 65536
N_BATCH = 128
N_TOWER = 4


def shared_direction(key):
    return jax.random.truncated_normal(key, -6.0, 6.0, (D,), jnp.float32)


def row_strength(top, power):
    position = jnp.arange(TOKENS, dtype=jnp.float32)[:, None] / TOKENS
    return top * position ** power


def embedding_rows(key, direction, top, power):
    noise = jax.random.truncated_normal(key, -6.0, 6.0, (TOKENS, D), jnp.float32)
    return noise + row_strength(top, power) * direction[None, :]


def draw_images(key, part):
    direction = shared_direction(key)
    key = jax.random.fold_in(key, 5)
    return embedding_rows(key, direction, 0.7, 1.0).astype(jnp.bfloat16)


def draw_texts(key, part):
    direction = shared_direction(key)
    key = jax.random.fold_in(key, 7)
    return embedding_rows(key, direction, 0.7, 1.0).astype(jnp.bfloat16)


def draw_block_mask(key, part):
    key = jax.random.fold_in(key, 11)
    n_blocks = BLK_GROUP * N_BATCH
    wide = WINDOW * BLK_GROUP
    breaks = jax.random.randint(key, (n_blocks,), 0, 6) == 0
    breaks = breaks.at[0].set(True)
    cluster = jnp.cumsum(breaks.astype(jnp.int32))
    blocks = jnp.arange(n_blocks, dtype=jnp.int32)
    target = (blocks // BLK_GROUP * BLK_GROUP)[:, None] + jnp.arange(wide, dtype=jnp.int32)[None, :]
    inside = target < n_blocks
    target_cluster = cluster[jnp.minimum(target, n_blocks - 1)]
    return (inside & (target_cluster == cluster[:, None])).astype(jnp.int32)


def draw_data_order(key, part):
    key = jax.random.fold_in(key, 23)
    devices = N_BATCH * N_TOWER
    per_pair = QUARTER // N_BATCH
    first_key, second_key = jax.random.split(key)
    local_perm = jax.vmap(lambda k: jax.random.permutation(k, QUARTER))(jax.random.split(first_key, devices)).astype(jnp.int32)
    slot_perm = jax.vmap(lambda k: jax.random.permutation(k, QUARTER))(jax.random.split(second_key, devices)).astype(jnp.int32)
    source = jnp.arange(devices, dtype=jnp.int32)[:, None]
    source_batch = source // N_TOWER
    source_tower = source % N_TOWER
    dest_batch = local_perm // per_pair
    slot_index = source_batch * per_pair + local_perm % per_pair
    dest_device = dest_batch * N_TOWER + source_tower
    placed = slot_perm[dest_device, slot_index]
    return (dest_device * QUARTER + placed).reshape(-1)


def setup_inputs(seed: int = 0) -> dict:
    streams_of = jax.random.split(jax.random.key(seed), 7)
    images = draw_images(jax.random.fold_in(streams_of[6], 71), 0)
    texts = draw_texts(jax.random.fold_in(streams_of[6], 71), 0)
    log_scale = jnp.clip(jax.random.uniform(streams_of[2], (), jnp.float32, 1.5, 3.0), 1.5, 3.0)
    bias = jnp.clip(jax.random.uniform(streams_of[3], (), jnp.float32, -2.0, 0.5), -2.0, 0.5)
    block_mask = draw_block_mask(jax.random.fold_in(streams_of[6], 71), 0)
    data_order = draw_data_order(jax.random.fold_in(streams_of[6], 71), 0)
    return dict(images=images, texts=texts, log_scale=log_scale, bias=bias, block_mask=block_mask, data_order=data_order)


NORM_EPS = 1e-06

def unit_rows(values):
    wide = values.astype(jnp.float32)
    inv_norm = lax.rsqrt(lax.optimization_barrier(jnp.sum(wide * wide, axis=-1, keepdims=True)) + NORM_EPS)
    return (wide * inv_norm, inv_norm)

def reference(images, texts, log_scale, bias, block_mask, data_order):
    rows_group = BLK_GROUP * BLOCK
    span = WINDOW * rows_group
    img_unit32, img_inv = unit_rows(images)
    img_unit = img_unit32.astype(jnp.bfloat16)
    txt_unit32, txt_inv = unit_rows(texts)
    txt_unit = txt_unit32.astype(jnp.bfloat16)
    padding = jnp.zeros(((WINDOW - 1) * rows_group, D), jnp.bfloat16)
    txt_padded = jnp.concatenate([txt_unit, padding], axis=0)
    logit_scale = jnp.exp(log_scale)
    positive = (jnp.arange(rows_group)[:, None] == jnp.arange(span)[None, :]).astype(jnp.float32)
    sign_of = 2.0 * positive - 1.0
    mask_groups = block_mask.reshape(N_BATCH, BLK_GROUP, WINDOW * BLK_GROUP).astype(jnp.float32)

    def one_group(carry, group):
        back_text, loss_sum, pair_count = carry
        start = (group * rows_group).astype(jnp.int32)
        img_rows = lax.dynamic_slice_in_dim(img_unit, start, rows_group, 0)
        candidates = lax.dynamic_slice_in_dim(txt_padded, start, span, 0)
        chosen = mask_groups[group]
        selected = jnp.repeat(jnp.repeat(chosen, BLOCK, axis=1), BLOCK, axis=0)
        logits = logit_scale * jnp.dot(img_rows, candidates.T, preferred_element_type=jnp.float32) + bias
        loss_sum = loss_sum + jnp.sum(selected * jax.nn.softplus(-sign_of * logits))
        pair_count = pair_count + jnp.sum(selected)
        coeffs = (selected * logit_scale * (jax.nn.sigmoid(logits) - positive)).astype(jnp.bfloat16)
        img_back = jnp.dot(coeffs, candidates, preferred_element_type=jnp.float32)
        txt_part = jnp.dot(coeffs.T, img_rows, preferred_element_type=jnp.float32)
        current = lax.dynamic_slice_in_dim(back_text, start, span, 0)
        back_text = lax.dynamic_update_slice_in_dim(back_text, current + txt_part, start, 0)
        return ((back_text, loss_sum, pair_count), img_back)
    start_carry = (jnp.zeros((TOKENS + (WINDOW - 1) * rows_group, D), jnp.float32), jnp.zeros((), jnp.float32), jnp.zeros((), jnp.float32))
    (back_text, loss_sum, pair_count), img_parts = lax.scan(one_group, start_carry, jnp.arange(N_BATCH, dtype=jnp.int32))
    img_back = img_parts.reshape(TOKENS, D)
    txt_back = back_text[:TOKENS]
    text_grad = (txt_back - txt_unit32 * lax.optimization_barrier(jnp.sum(txt_unit32 * txt_back, axis=-1, keepdims=True))) * txt_inv
    img_local = (img_back - img_unit32 * lax.optimization_barrier(jnp.sum(img_unit32 * img_back, axis=-1, keepdims=True))) * img_inv
    image_grad = jnp.zeros((TOKENS, D), jnp.float32).at[data_order.astype(jnp.int32)].set(img_local)
    return (image_grad, text_grad, loss_sum / pair_count)
```

```python
import functools

import jax
import jax.numpy as jnp
from jax import lax
from jax.experimental import pallas as pl
from jax.experimental.pallas import tpu as pltpu
from jax.sharding import PartitionSpec as P

NORM_EPS = 1e-06
MESH = pl.DeviceIdType.MESH
LANES = 128
TOP = 32760.0
LOG_STEP = 0.6931471805599453 / 256.0
NT = (((1,), (1,)), ((), ()))
TN = (((0,), (0,)), ((), ()))
NN = (((1,), (0,)), ((), ()))


def mxu(a, b, dims):
    return lax.dot_general(a, b, dims, preferred_element_type=jnp.float32)


def row_inv(wide):
    return lax.rsqrt(jnp.sum(wide * wide, axis=-1, keepdims=True) + NORM_EPS)


def as_codes(rows):
    top = jnp.maximum(jnp.max(jnp.abs(rows), axis=-1, keepdims=True), 1e-30)
    power = jnp.ceil(jnp.log(top) * (1.0 / LOG_STEP))
    codes = jnp.round(rows * (TOP * jnp.exp(power * -LOG_STEP))).astype(jnp.int32)
    return codes, power.astype(jnp.int32)


def step_of(power):
    return jnp.exp(power.astype(jnp.float32) * LOG_STEP) * (1.0 / TOP)


def lane_ids(rows):
    return lax.broadcasted_iota(jnp.int32, (rows, LANES), 1)


def words_of(codes, extras):
    low = [codes[:, LANES * (k + 4) : LANES * (k + 5)] for k in range(4)] + [extras]
    order = (0, 1, 2, 3, 8)
    return [
        (codes[:, LANES * k : LANES * (k + 1)] << 16) | (other & 0xFFFF)
        for k, other in zip(order, low, strict=True)
    ]


def high_of(word):
    return word >> 16


def low_of(word):
    return (word << 16) >> 16


def columns_of(words, high, low):
    return [high(words[k]) for k in range(4)] + [low(words[k]) for k in range(4)] + [high(words[4])]


def rows_from(ref):
    words = [ref[:, LANES * k : LANES * (k + 1)] for k in range(5)]
    extras = low_of(words[4])
    codes = jnp.concatenate(columns_of(words, high_of, low_of), axis=1)
    return codes.astype(jnp.float32) * step_of(extras[:, 0:1]), extras


def loss_fields(total):
    power = jnp.ceil(jnp.log(jnp.maximum(total, 1e-30)) * (1.0 / 0.6931471805599453))
    scaled = total * jnp.exp(power * -0.6931471805599453) * 8192.0
    first = jnp.floor(scaled)
    second = jnp.floor((scaled - first) * 16384.0)
    return [v.astype(jnp.int32) for v in (power, first, second)]


def loss_from(power, first, second):
    wide = first.astype(jnp.float32) + second.astype(jnp.float32) * (1.0 / 16384.0)
    return wide * jnp.exp(power.astype(jnp.float32) * 0.6931471805599453) * (1.0 / 8192.0)


def kernel(
    images_ref,
    texts_ref,
    log_scale_ref,
    bias_ref,
    mask_ref,
    order_ref,
    image_grad_ref,
    text_grad_ref,
    loss_ref,
    img_unit,
    img_inv,
    cand,
    coeffs,
    loss_acc,
    own_text,
    own_image,
    part_send,
    part_recv,
    tower_send,
    tower_recv,
    row_send,
    row_recv,
    cand_sent,
    cand_here,
    part_sent,
    part_here,
    tower_sent,
    tower_here,
    row_sent,
    row_here,
    row_own,
):
    n_batch = lax.axis_size("batch")
    n_tower = lax.axis_size("tower")
    me = lax.axis_index("batch")
    tower = lax.axis_index("tower")
    core = lax.rem(me, 2)
    quarter, width = texts_ref.shape

    def batch_at(offset):
        return lax.rem(me + (n_batch + offset), n_batch)

    def tower_at(offset):
        return lax.rem(tower + offset, n_tower)

    barrier = pltpu.get_barrier_semaphore()

    def greet(i, _):
        pl.semaphore_signal(
            barrier, 1, device_id={"batch": lax.rem(me + i, n_batch)}, device_id_type=MESH
        )
        return 0

    lax.fori_loop(1, n_batch, greet, 0)
    for d in range(1, n_tower):
        pl.semaphore_signal(barrier, 1, device_id={"tower": tower_at(d)}, device_id_type=MESH)

    wide = texts_ref[...].astype(jnp.float32)
    txt_inv = row_inv(wide)
    cand[0] = (wide * txt_inv).astype(jnp.bfloat16)

    pl.semaphore_wait(barrier, n_batch - 1 + n_tower - 1)

    def cand_copy(source, target, dest, sem):
        return pltpu.make_async_remote_copy(
            src_ref=cand.at[source],
            dst_ref=cand.at[target],
            send_sem=cand_sent.at[sem],
            recv_sem=cand_here.at[target],
            device_id={"batch": dest},
            device_id_type=MESH,
        )

    first_slot = 3 - 2 * core
    sibling = me + 1 - 2 * core
    outward = cand_copy(0, 1 + 2 * core, batch_at(-1 - 2 * core), 0)
    outward.start()

    @pl.when(core == 1)
    def _():
        cand_copy(0, 1, sibling, 1).start()

    def norm(q, _):
        rows = pl.ds(q * quarter, quarter)
        values = images_ref[rows, :].astype(jnp.float32)
        inv = row_inv(values)
        img_inv[rows, :] = inv
        img_unit[rows, :] = (values * inv).astype(jnp.bfloat16)
        return 0

    lax.fori_loop(0, n_tower, norm, 0)

    logit_scale = jnp.exp(jnp.full((1, LANES), log_scale_ref[0], jnp.float32))
    bias = bias_ref[0]
    loss_acc[...] = jnp.zeros_like(loss_acc)
    diagonal = lax.broadcasted_iota(jnp.int32, (quarter, quarter), 0) == lax.broadcasted_iota(
        jnp.int32, (quarter, quarter), 1
    )

    def pairs(k, own):
        block = cand[k]

        def some(q, _):
            rows = pl.ds(pl.multiple_of(q * quarter, quarter), quarter)
            logits = logit_scale * mxu(img_unit[rows, :], block, NT) + bias
            small = jnp.exp(-jnp.abs(logits))
            share = 1.0 / (1.0 + small)
            sigmoid = jnp.where(logits >= 0.0, share, small * share)
            loss = jnp.maximum(logits, 0.0) + jnp.log1p(small)
            chosen = mask_ref[q // 2, 2 * k + tower // 2].astype(jnp.float32)
            if own:
                positive = jnp.where(diagonal & (q == tower), 1.0, 0.0)
                loss = loss - positive * logits
                sigmoid = sigmoid - positive
            loss_acc[...] += chosen * loss
            cols = pl.ds(pl.multiple_of(k * quarter, quarter), quarter)
            coeffs[rows, cols] = (chosen * logit_scale * sigmoid).astype(jnp.bfloat16)
            return 0

        lax.fori_loop(0, n_tower, some, 0)

    def text_part(k):
        cols = pl.ds(pl.multiple_of(k * quarter, quarter), quarter)
        return mxu(coeffs[:, cols], img_unit[...], TN)

    def put_words(ref, slot, codes, extras):
        for j, word in enumerate(words_of(codes, extras)):
            ref[slot, :, LANES * j : LANES * (j + 1)] = word

    def part_copy(k):
        return pltpu.make_async_remote_copy(
            src_ref=part_send.at[k - 1],
            dst_ref=part_recv.at[k - 1],
            send_sem=part_sent.at[k - 1],
            recv_sem=part_here.at[k - 1],
            device_id={"batch": batch_at(k)},
            device_id_type=MESH,
        )

    def text_part_out(k):
        codes, power = as_codes(text_part(k))
        put_words(part_send, k - 1, codes, jnp.where(lane_ids(quarter) == 0, power, 0))
        part_copy(k).start()

    pairs(0, True)
    own_text[...] = text_part(0)

    cand_copy(0, first_slot, me, 0).wait_recv()
    cand_copy(first_slot, 2, sibling, 2).start()

    @pl.when(core == 1)
    def _():
        cand_copy(1, 3, batch_at(-2), 3).start()

    pairs(first_slot, False)
    text_part_out(first_slot)
    second_slot = 1 + core
    cand_copy(0, second_slot, me, 0).wait_recv()
    pairs(second_slot, False)
    text_part_out(second_slot)
    third_slot = 2 + core
    cand_copy(0, third_slot, me, 0).wait_recv()
    pairs(third_slot, False)

    total = jnp.sum(jnp.sum(loss_acc[...], axis=1, keepdims=True), axis=0, keepdims=True)

    def image_part(q):
        rows = pl.ds(pl.multiple_of(q * quarter, quarter), quarter)
        back = mxu(coeffs[rows, :], cand[...].reshape(4 * quarter, width), NN)
        inv = img_inv[rows, :]
        unit = images_ref[rows, :].astype(jnp.float32) * inv
        return (back - unit * jnp.sum(unit * back, axis=-1, keepdims=True)) * inv

    def fields(head, rest):
        lane = lane_ids(quarter)
        out = jnp.where(lane == 0, head, 0)
        for j, value in enumerate(rest):
            out = jnp.where(lane == j + 1, value, out)
        return out

    def tower_copy(d):
        return pltpu.make_async_remote_copy(
            src_ref=tower_send.at[d - 1],
            dst_ref=tower_recv.at[d - 1],
            send_sem=tower_sent.at[d - 1],
            recv_sem=tower_here.at[d - 1],
            device_id={"tower": tower_at(d)},
            device_id_type=MESH,
        )

    loss_parts = loss_fields(total)
    for d in (2, 1, 3):
        codes, power = as_codes(image_part(tower_at(d)))
        put_words(tower_send, d - 1, codes, fields(power, loss_parts))
        tower_copy(d).start()

    text_part_out(third_slot)
    own_image[...] = image_part(tower)

    grad = own_image[...]
    for d in (1, 3, 2):
        tower_copy(d).wait_recv()
        rows, extras = rows_from(tower_recv.at[d - 1])
        grad = grad + rows
        total = total + loss_from(extras[0:1, 1:2], extras[0:1, 2:3], extras[0:1, 3:4])
    codes, power = as_codes(grad)
    order = order_ref[...]
    picks = lax.broadcasted_iota(jnp.int32, (quarter, quarter), 0) == order // (n_tower * quarter)
    slots = jnp.sum(jnp.where(picks, lax.rem(order, quarter), 0), axis=1, keepdims=True)
    one_hot = jnp.where(picks, 1.0, 0.0).astype(jnp.bfloat16)

    def bytes_of(whole):
        return whole.astype(jnp.float32).astype(jnp.bfloat16)

    def moved(matrix, high, low, dims):
        return mxu(matrix, bytes_of(high), dims) * 256.0 + mxu(matrix, bytes_of(low), dims)

    def moved_whole(whole):
        return moved(one_hot, whole >> 8, whole & 0xFF, NN).astype(jnp.int32)

    count = mask_ref[0, 0] * 0
    for p in range(mask_ref.shape[0]):
        for c in range(mask_ref.shape[1]):
            count = count + mask_ref[p, c]
    sent_power = moved_whole(jnp.where(lane_ids(quarter) == 0, power, 0))
    extras = sent_power
    for j, value in enumerate([slots, count, *loss_fields(total)]):
        extras = jnp.where(lane_ids(quarter) == j + 1, value, extras)
    for j, word in enumerate(words_of(moved_whole(codes), extras)):
        for g in range(quarter // 8):
            row_send[pl.ds(40 * g + j, 8, stride=5), :] = word[8 * g : 8 * (g + 1), :]

    def row_copy(dest):
        return pltpu.make_async_remote_copy(
            src_ref=row_send.at[pl.ds(dest * 5, 5)],
            dst_ref=row_recv.at[pl.ds(me * 5, 5)],
            send_sem=row_sent,
            recv_sem=row_here,
            device_id={"batch": dest},
            device_id_type=MESH,
        )

    def send_row(i, _):
        half = (i + 1) // 2
        offset = n_batch // 2 + half * (1 - 2 * lax.rem(i, 2))
        row_copy(lax.rem(me + offset, n_batch)).start()
        return 0

    lax.fori_loop(0, n_batch - 1, send_row, 0)
    here = pl.ds(me * 5, 5)
    own_copy = pltpu.make_async_copy(row_send.at[here], row_recv.at[here], row_own)
    own_copy.start()

    back = own_text[...]
    for k in (1, 2, 3):
        part_copy(k).wait_recv()
        rows, _ = rows_from(part_recv.at[k - 1])
        back = back + rows
    wide = texts_ref[...].astype(jnp.float32)
    inv = row_inv(wide)
    unit = wide * inv
    text_grad_ref[...] = (back - unit * jnp.sum(unit * back, axis=-1, keepdims=True)) * inv

    own_copy.wait()
    all_rows = row_recv.at[pl.ds(0, (n_batch - 1) * 5)]
    pltpu.make_async_copy(all_rows, all_rows, row_here).wait()
    words = [
        jnp.concatenate(
            [row_recv[pl.ds(40 * g + j, 8, stride=5), :] for g in range(quarter // 8)], axis=0
        )
        for j in range(5)
    ]
    extras = low_of(words[4])
    places = jnp.where(lane_ids(quarter) == extras[:, 1:2], 1.0, 0.0).astype(jnp.bfloat16)
    steps = moved(places, extras >> 8, extras & 0xFF, TN)[:, 0:1]
    steps = jnp.exp(steps * LOG_STEP) * (1.0 / TOP)
    parts = columns_of(words, high_of, low_of)
    for j, whole in enumerate(parts):
        image_grad_ref[:, LANES * j : LANES * (j + 1)] = (
            moved(places, whole >> 8, whole & 0xFF, TN) * steps
        )
    losses = loss_from(extras[:, 3:4], extras[:, 4:5], extras[:, 5:6])
    counts = extras[:, 2:3].astype(jnp.float32) * float(4 * quarter * quarter)
    loss_ref[...] = jnp.sum(losses, axis=0, keepdims=True) / jnp.sum(
        counts, axis=0, keepdims=True
    )

    outward.wait_send()
    cand_copy(first_slot, 2, sibling, 2).wait_send()

    @pl.when(core == 1)
    def _():
        cand_copy(0, 1, sibling, 1).wait_send()
        cand_copy(1, 3, batch_at(-2), 3).wait_send()

    for k in (1, 2, 3):
        part_copy(k).wait_send()
        tower_copy(k).wait_send()
    all_sent = row_send.at[pl.ds(0, (n_batch - 1) * 5)]
    pltpu.make_async_copy(all_sent, all_sent, row_sent).wait()


def shards(images, texts, log_scale, bias, block_mask, data_order):
    rows_group, width = images.shape
    quarter = texts.shape[0]
    words = 5 * LANES
    vmem = pl.BlockSpec(memory_space=pltpu.VMEM)
    smem = pl.BlockSpec(memory_space=pltpu.SMEM)
    dma = pltpu.SemaphoreType.DMA
    image_grad, text_grad, pair_loss = pl.pallas_call(
        kernel,
        out_shape=(
            jax.ShapeDtypeStruct((quarter, width), jnp.float32),
            jax.ShapeDtypeStruct((quarter, width), jnp.float32),
            jax.ShapeDtypeStruct((1, 1), jnp.float32),
        ),
        in_specs=[vmem, vmem, smem, smem, smem, vmem],
        out_specs=(vmem, vmem, vmem),
        scratch_shapes=[
            pltpu.VMEM((rows_group, width), jnp.bfloat16),
            pltpu.VMEM((rows_group, 1), jnp.float32),
            pltpu.VMEM((4, quarter, width), jnp.bfloat16),
            pltpu.VMEM((rows_group, 4 * quarter), jnp.bfloat16),
            pltpu.VMEM((quarter, quarter), jnp.float32),
            pltpu.VMEM((quarter, width), jnp.float32),
            pltpu.VMEM((quarter, width), jnp.float32),
            pltpu.VMEM((3, quarter, words), jnp.int32),
            pltpu.VMEM((3, quarter, words), jnp.int32),
            pltpu.VMEM((3, quarter, words), jnp.int32),
            pltpu.VMEM((3, quarter, words), jnp.int32),
            pltpu.VMEM((quarter * 5, LANES), jnp.int32),
            pltpu.VMEM((quarter * 5, LANES), jnp.int32),
            dma((4,)),
            dma((4,)),
            dma((3,)),
            dma((3,)),
            dma((3,)),
            dma((3,)),
            dma,
            dma,
            dma,
        ],
        compiler_params=pltpu.CompilerParams(
            collective_id=0, has_side_effects=True, vmem_limit_bytes=48 * 1024 * 1024
        ),
    )(
        images,
        texts,
        log_scale.reshape(1),
        bias.reshape(1),
        block_mask,
        data_order.reshape(1, quarter),
    )
    return image_grad, text_grad, pair_loss.reshape(())


def solution(mesh):
    in_specs = (
        P("batch", None),
        P(("batch", "tower"), None),
        P(),
        P(),
        P("batch", None),
        P(("batch", "tower")),
    )
    out_specs = (P(("batch", "tower"), None), P(("batch", "tower"), None), P())
    return jax.shard_map(shards, mesh=mesh, in_specs=in_specs, out_specs=out_specs, check_vma=False)
```

```python
import functools

import jax
import jax.numpy as jnp
from jax import lax
from jax.experimental import pallas as pl
from jax.experimental.pallas import tpu as pltpu
from jax.sharding import PartitionSpec as P

NORM_EPS = 1e-06
MESH = pl.DeviceIdType.MESH
LANES = 128
TOP = 32760.0
LOG_STEP = 0.6931471805599453 / 256.0
NT = (((1,), (1,)), ((), ()))
TN = (((0,), (0,)), ((), ()))
NN = (((1,), (0,)), ((), ()))


def mxu(a, b, dims):
    return lax.dot_general(a, b, dims, preferred_element_type=jnp.float32)


def row_inv(wide):
    return lax.rsqrt(jnp.sum(wide * wide, axis=-1, keepdims=True) + NORM_EPS)


def as_codes(rows):
    top = jnp.maximum(jnp.max(jnp.abs(rows), axis=-1, keepdims=True), 1e-30)
    power = jnp.ceil(jnp.log(top) * (1.0 / LOG_STEP))
    codes = jnp.round(rows * (TOP * jnp.exp(power * -LOG_STEP))).astype(jnp.int32)
    return codes, power.astype(jnp.int32)


def step_of(power):
    return jnp.exp(power.astype(jnp.float32) * LOG_STEP) * (1.0 / TOP)


def lane_ids(rows):
    return lax.broadcasted_iota(jnp.int32, (rows, LANES), 1)


def words_of(codes, extras):
    group = [codes[:, LANES * k : LANES * (k + 1)] for k in range(9)]
    pairs = [(group[8], extras)] + [(group[k], group[k + 4]) for k in range(4)]
    return [word_of(high, low) for high, low in pairs]


def word_of(high, low):
    return (high << 16) | (low & 0xFFFF)


def high_of(word):
    return word >> 16


def low_of(word):
    return (word << 16) >> 16


def loss_fields(total):
    power = jnp.ceil(jnp.log(jnp.maximum(total, 1e-30)) * (1.0 / 0.6931471805599453))
    scaled = total * jnp.exp(power * -0.6931471805599453) * 8192.0
    first = jnp.floor(scaled)
    second = jnp.floor((scaled - first) * 16384.0)
    return [v.astype(jnp.int32) for v in (power, first, second)]


def loss_from(power, first, second):
    wide = first.astype(jnp.float32) + second.astype(jnp.float32) * (1.0 / 16384.0)
    return wide * jnp.exp(power.astype(jnp.float32) * 0.6931471805599453) * (1.0 / 8192.0)


PLANE = 8
SUM_PARTS = ((0, 2), (2, 3), (3, 4), (4, 5))
ROW_PARTS = ((0, 1), (1, 2), (2, 3), (3, 5))


def kernel(
    images_hbm,
    texts_hbm,
    log_scale_ref,
    bias_ref,
    mask_ref,
    order_hbm,
    image_grad_ref,
    text_grad_ref,
    loss_ref,
    images_ref,
    texts_ref,
    order_ref,
    img_unit,
    img_inv,
    cand,
    coeffs,
    dots,
    loss_acc,
    own_text,
    own_image,
    core_send,
    core_recv,
    part_send,
    part_recv,
    tower_send,
    tower_recv,
    tower_relay,
    row_send,
    row_mid,
    row_recv,
    in_here,
    cand_sent,
    cand_here,
    core_sent,
    core_here,
    part_sent,
    part_here,
    hop_sent,
    hop_here,
    near_sent,
    near_here,
    far_sent,
    far_here,
    plane_sent,
    plane_here,
    row_sent,
    row_here,
    row_own,
):
    n_batch = lax.axis_size("batch")
    n_tower = lax.axis_size("tower")
    n_z = n_batch // PLANE
    me = lax.axis_index("batch")
    tower = lax.axis_index("tower")
    z = me // PLANE
    j = lax.rem(me, PLANE)
    core = lax.rem(me, 2)
    sibling = me + 1 - 2 * core
    quarter, width = texts_ref.shape
    half = quarter // 2

    def batch_at(offset):
        return lax.rem(me + (n_batch + offset), n_batch)

    def tower_at(offset):
        return lax.rem(tower + offset, n_tower)

    def z_step(i):
        return n_z // 2 + ((i + 1) // 2) * (1 - 2 * lax.rem(i, 2))

    def column_at(i):
        return lax.rem(z + z_step(i), n_z) * PLANE + j

    def remote(source, target, sent, here, dest):
        return pltpu.make_async_remote_copy(
            src_ref=source,
            dst_ref=target,
            send_sem=sent,
            recv_sem=here,
            device_id=dest,
            device_id_type=MESH,
        )

    loads = [
        pltpu.make_async_copy(texts_hbm, texts_ref, in_here.at[0]),
        pltpu.make_async_copy(images_hbm, images_ref, in_here.at[1]),
        pltpu.make_async_copy(order_hbm, order_ref, in_here.at[2]),
    ]
    for load in loads:
        load.start()

    chips = n_batch // 2
    relay_to = z * PLANE + lax.rem(j + 2, PLANE)
    relayed = lax.rem(z * (PLANE // 2) + lax.rem(j // 2 + 3, PLANE // 2) + chips - 2, chips) * 2 + 1
    chip_after = lax.rem(me // 2 + 2, chips)
    relay_from = ((chip_after // 4) * 4 + lax.rem(lax.rem(chip_after, 4) + 1, 4)) * 2

    barrier = pltpu.get_barrier_semaphore()

    def greet(dest):
        pl.semaphore_signal(barrier, 1, device_id=dest, device_id_type=MESH)

    def greet_column(i, _):
        greet({"batch": column_at(i)})
        return 0

    def greet_plane(i, _):
        greet({"batch": z * PLANE + lax.rem(j + i, PLANE)})
        return 0

    lax.fori_loop(0, n_z - 1, greet_column, 0)
    greet({"tower": tower_at(1)})
    greet({"tower": tower_at(n_tower - 1)})

    @pl.when(core == 0)
    def _():
        greet({"batch": batch_at(3)})
        greet({"batch": batch_at(-1)})

    @pl.when(core == 1)
    def _():
        greet({"batch": relay_from})
        for d in (-3, 1, 2, -2):
            greet({"batch": batch_at(d)})

    lax.fori_loop(1, PLANE, greet_plane, 0)

    loads[0].wait()
    wide = texts_ref[...].astype(jnp.float32)
    cand[0] = (wide * row_inv(wide)).astype(jnp.bfloat16)

    pl.semaphore_wait(barrier, n_z - 1 + PLANE - 1 + 2 + 3 + core)

    def cand_copy(source, target, dest, sem):
        return remote(
            cand.at[source], cand.at[target], cand_sent.at[sem], cand_here.at[target], {"batch": dest}
        )

    outward = cand_copy(0, 3 - 2 * (1 - core), batch_at(-1 - 2 * core), 0)
    to_sibling = cand_copy(0, 1, sibling, 1)
    to_relay = cand_copy(0, 4, relay_to, 1)
    pass_far = cand_copy(4, 3, relayed, 2)
    pass_near = cand_copy(3 - 2 * core, 2, sibling, 3)

    @pl.when(core == 0)
    def _():
        to_relay.start()

    outward.start()

    @pl.when(core == 1)
    def _():
        to_sibling.start()

    loads[1].wait()

    def norm(q, _):
        rows = pl.ds(q * quarter, quarter)
        values = images_ref[rows, :].astype(jnp.float32)
        inv = row_inv(values)
        img_inv[rows, :] = inv
        img_unit[rows, :] = (values * inv).astype(jnp.bfloat16)
        return 0

    lax.fori_loop(0, n_tower, norm, 0)

    logit_scale = jnp.exp(jnp.full((1, LANES), log_scale_ref[0], jnp.float32))
    bias = bias_ref[0]
    loss_acc[...] = jnp.zeros_like(loss_acc)
    diagonal = lax.broadcasted_iota(jnp.int32, (quarter, quarter), 0) == lax.broadcasted_iota(
        jnp.int32, (quarter, quarter), 1
    )

    def pairs(k, own):
        dots[...] = mxu(img_unit[...], cand[k], NT)

        def some(q, _):
            rows = pl.ds(pl.multiple_of(q * quarter, quarter), quarter)
            logits = logit_scale * dots[rows, :] + bias
            small = jnp.exp(-jnp.abs(logits))
            share = 1.0 / (1.0 + small)
            sigmoid = jnp.where(logits >= 0.0, share, small * share)
            loss = jnp.maximum(logits, 0.0) + jnp.log1p(small)
            chosen = mask_ref[q // 2, 2 * k + tower // 2].astype(jnp.float32)
            if own:
                positive = jnp.where(diagonal & (q == tower), 1.0, 0.0)
                loss = loss - positive * logits
                sigmoid = sigmoid - positive
            loss_acc[...] += chosen * loss
            cols = pl.ds(pl.multiple_of(k * quarter, quarter), quarter)
            coeffs[rows, cols] = (chosen * logit_scale * sigmoid).astype(jnp.bfloat16)
            return 0

        lax.fori_loop(0, n_tower, some, 0)

    def text_part(k):
        cols = pl.ds(pl.multiple_of(k * quarter, quarter), quarter)
        return mxu(coeffs[:, cols], img_unit[...], TN)

    def fields(values, rows):
        out = jnp.zeros((rows, LANES), jnp.int32)
        for n, value in enumerate(values):
            out = jnp.where(lane_ids(rows) == n, value, out)
        return out

    def put_rows(ref, rows, more):
        codes, power = as_codes(rows)
        for n, word in enumerate(words_of(codes, fields([power, *more], rows.shape[0]))):
            ref[:, LANES * n : LANES * (n + 1)] = word

    def get_rows(ref):
        words = [ref[:, LANES * n : LANES * (n + 1)] for n in range(5)]
        codes = [high_of(w) for w in words[1:]] + [low_of(w) for w in words[1:]] + [high_of(words[0])]
        step = step_of(low_of(words[0])[:, 0:1])
        return jnp.concatenate(codes, axis=1).astype(jnp.float32) * step

    pairs(0, True)
    own_text[...] = text_part(0)

    @pl.when(core == 0)
    def _():
        cand_copy(0, 4, me, 0).wait_recv()
        pass_far.start()

    cand_copy(0, 1, me, 0).wait_recv()

    @pl.when(core == 1)
    def _():
        pass_near.start()

    pairs(1, False)

    def core_copy(n):
        return remote(
            core_send.at[n], core_recv.at[n], core_sent.at[n], core_here.at[n], {"batch": sibling}
        )

    @pl.when(core == 0)
    def _():
        core_send[0] = text_part(1)
        core_copy(0).start()

    second_slot = 3 - core
    third_slot = 2 + core
    cand_copy(0, second_slot, me, 0).wait_recv()

    @pl.when(core == 0)
    def _():
        pass_near.start()

    pairs(second_slot, False)
    cand_copy(0, third_slot, me, 0).wait_recv()
    pairs(third_slot, False)

    total = jnp.sum(jnp.sum(loss_acc[...], axis=1, keepdims=True), axis=0, keepdims=True)

    def image_part(q):
        rows = pl.ds(pl.multiple_of(q * quarter, quarter), quarter)
        texts = cand[0:4].reshape(4 * quarter, width)
        back = mxu(coeffs[rows, :], texts, NN)
        inv = img_inv[rows, :]
        unit = images_ref[rows, :].astype(jnp.float32) * inv
        return (back - unit * jnp.sum(unit * back, axis=-1, keepdims=True)) * inv

    def cut(part):
        first, last = SUM_PARTS[part]
        return pl.ds(first * LANES, (last - first) * LANES)

    def hop_copy(part, way):
        return remote(
            tower_send.at[1, pl.ds(way * half, half), cut(part)],
            tower_relay.at[way, :, cut(part)],
            hop_sent.at[part, way],
            hop_here.at[part, way],
            {"tower": tower_at(1 + 2 * way)},
        )

    def near_copy(part, way):
        return remote(
            tower_send.at[2 * way, :, cut(part)],
            tower_recv.at[2 * way, :, cut(part)],
            near_sent.at[part, way],
            near_here.at[part, way],
            {"tower": tower_at(1 + 2 * way)},
        )

    def far_copy(part, way):
        return remote(
            tower_relay.at[way, :, cut(part)],
            tower_recv.at[1, pl.ds(way * half, half), cut(part)],
            far_sent.at[part, way],
            far_here.at[part, way],
            {"tower": tower_at(1 + 2 * way)},
        )

    def start_both(copy, part):
        if part < len(SUM_PARTS):
            for way in (0, 1):
                copy(part, way).start()

    loss_parts = loss_fields(total)
    put_rows(tower_send.at[1], image_part(tower_at(2)), loss_parts)
    start_both(hop_copy, 0)
    for way in (0, 1):
        put_rows(tower_send.at[2 * way], image_part(tower_at(1 + 2 * way)), loss_parts)
        near_copy(0, way).start()
    start_both(hop_copy, 1)

    def part_copy(n, dest):
        return remote(
            part_send.at[n], part_recv.at[n], part_sent.at[n], part_here.at[n], {"batch": dest}
        )

    far_part = part_copy(0, batch_at(2))
    near_part = part_copy(1, batch_at(3 - 2 * core))

    @pl.when(core == 1)
    def _():
        put_rows(part_send.at[0], text_part(3), [])
        far_part.start()

    core_send[1] = text_part(2)
    core_copy(1).start()
    own_image[...] = image_part(tower)

    order = order_ref
    loads[2].wait()
    place = lax.broadcasted_iota(jnp.int32, (quarter, quarter), 0)
    goal = lax.rem(z + z_step(lax.rem(place, n_z)), n_z) * PLANE + place // n_z
    picks = goal == order[...] // (n_tower * quarter)
    slots = jnp.sum(jnp.where(picks, lax.rem(order[...], quarter), 0), axis=1, keepdims=True)
    one_hot = jnp.where(picks, 1.0, 0.0).astype(jnp.bfloat16)

    def bytes_of(whole):
        return whole.astype(jnp.float32).astype(jnp.bfloat16)

    def moved(matrix, whole, dims):
        high, low = bytes_of(whole >> 8), bytes_of(whole & 0xFF)
        return mxu(matrix, high, dims) * 256.0 + mxu(matrix, low, dims)

    count = mask_ref[0, 0] * 0
    for p in range(mask_ref.shape[0]):
        for c in range(mask_ref.shape[1]):
            count = count + mask_ref[p, c]

    def plane_copy(part, peer):
        first, last = ROW_PARTS[part]
        return remote(
            row_send.at[pl.ds(first, last - first), peer],
            row_mid.at[pl.ds(first, last - first), j],
            plane_sent,
            plane_here.at[part],
            {"batch": z * PLANE + peer},
        )

    def column_copy(part, i):
        first, last = ROW_PARTS[part]
        here = row_mid.at[pl.ds(first, last - first), :, pl.ds(i, 1), :]
        there = row_recv.at[pl.ds(first, last - first), :, pl.ds(i, 1), :]
        return remote(here, there, row_sent, row_here, {"batch": column_at(i)})

    def to_plane(part):
        first, last = ROW_PARTS[part]

        def some(i, _):
            plane_copy(part, lax.rem(j + i, PLANE)).start()
            return 0

        lax.fori_loop(1, PLANE, some, 0)
        for n in range(first, last):
            row_mid[n, pl.ds(j, 1)] = row_send[n, pl.ds(j, 1)]

    def to_column(part):
        first, last = ROW_PARTS[part]
        others = row_mid.at[pl.ds(first, last - first), pl.ds(0, PLANE - 1)]
        pltpu.make_async_copy(others, others, plane_here.at[part]).wait()

        def some(i, _):
            column_copy(part, i).start()
            return 0

        lax.fori_loop(0, n_z - 1, some, 0)

    def text_sums(which):
        @pl.when(core == which)
        def _():
            core_copy(1).wait_recv()
            rest = text_part(3 - 2 * which) + core_recv[1]
            if which == 1:
                far_part.wait_recv()
                rest = rest + get_rows(part_recv.at[0])
            put_rows(part_send.at[1], rest, [])
            near_part.start()

    def pass_on(part):
        if part < len(SUM_PARTS):
            for way in (0, 1):
                hop_copy(part, way).wait_recv()
                far_copy(part, way).start()
        start_both(near_copy, part + 1)
        start_both(hop_copy, part + 2)

    powers = []
    steps = []
    spare = None
    for part, (first, last) in enumerate(SUM_PARTS):
        if part == 0:
            pass_on(0)
            text_sums(0)
            pass_on(1)
        for way in (0, 1):
            near_copy(part, way).wait_recv()
            far_copy(part, way).wait_recv()
        if part == 0:
            for n in range(3):
                extras = low_of(tower_recv[n, :, 0:LANES])
                steps.append(step_of(extras[:, 0:1]))
                total = total + loss_from(extras[0:1, 1:2], extras[0:1, 2:3], extras[0:1, 3:4])
            spare = own_image[:, 8 * LANES :]
            for n in range(3):
                spare = spare + high_of(tower_recv[n, :, 0:LANES]).astype(jnp.float32) * steps[n]
        rows = []
        for group in range(max(first, 1), last):
            high = own_image[:, (group - 1) * LANES : group * LANES]
            low = own_image[:, (group + 3) * LANES : (group + 4) * LANES]
            for n in range(3):
                word = tower_recv[n, :, group * LANES : (group + 1) * LANES]
                high = high + high_of(word).astype(jnp.float32) * steps[n]
                low = low + low_of(word).astype(jnp.float32) * steps[n]
            rows += [high, low]
        final = part == len(SUM_PARTS) - 1
        if final:
            rows.append(spare)
        codes, power = as_codes(jnp.concatenate(rows, axis=1))
        powers.append(power)
        if final:
            codes = jnp.concatenate([codes, fields(powers, quarter)], axis=1)
        codes = moved(one_hot, codes, NN).astype(jnp.int32)
        groups = [codes[:, LANES * n : LANES * (n + 1)] for n in range(codes.shape[1] // LANES)]
        if final:
            for n, value in enumerate([slots, count, *loss_fields(total)]):
                groups[-1] = jnp.where(lane_ids(quarter) == len(powers) + n, value, groups[-1])
        for n in range(len(groups) // 2):
            word = word_of(groups[2 * n], groups[2 * n + 1])
            row_send[ROW_PARTS[part][0] + n] = word.reshape(PLANE, n_z, LANES)
        to_plane(part)
        pass_on(part + 2)
        if part == 0:
            text_sums(1)
        to_column(part)

    own_here = row_mid.at[:, :, pl.ds(n_z - 1, 1), :]
    own_there = row_recv.at[:, :, pl.ds(n_z - 1, 1), :]
    own_copy = pltpu.make_async_copy(own_here, own_there, row_own)
    own_copy.start()

    near_part.wait_recv()
    own_text[...] += get_rows(part_recv.at[1])

    @pl.when(core == 1)
    def _():
        core_copy(0).wait_recv()
        own_text[...] += core_recv[0]

    back = own_text[...]
    wide = texts_ref[...].astype(jnp.float32)
    inv = row_inv(wide)
    unit = wide * inv
    text_grad_ref[...] = (back - unit * jnp.sum(unit * back, axis=-1, keepdims=True)) * inv

    own_copy.wait()
    all_rows = row_recv.at[:, :, pl.ds(0, n_z - 1), :]
    pltpu.make_async_copy(all_rows, all_rows, row_here).wait()
    words = [row_recv[n].reshape(quarter, LANES) for n in range(5)]
    extras = low_of(words[4])
    n_powers = len(powers)
    places = jnp.where(lane_ids(quarter) == extras[:, n_powers : n_powers + 1], 1.0, 0.0)
    places = places.astype(jnp.bfloat16)
    sizes = jnp.exp(moved(places, extras, TN) * LOG_STEP) * (1.0 / TOP)

    def put_group(group, whole, part):
        image_grad_ref[:, LANES * group : LANES * (group + 1)] = (
            moved(places, whole, TN) * sizes[:, part : part + 1]
        )

    for part, (first, last) in enumerate(ROW_PARTS):
        for n in range(first, min(last, 4)):
            put_group(n, high_of(words[n]), part)
            put_group(n + 4, low_of(words[n]), part)
    put_group(8, high_of(words[4]), len(ROW_PARTS) - 1)
    tail = [extras[:, n_powers + n : n_powers + n + 1] for n in range(1, 5)]
    losses = jnp.sum(loss_from(*tail[1:]), axis=0, keepdims=True)
    counts = jnp.sum(tail[0].astype(jnp.float32), axis=0, keepdims=True)
    loss_ref[...] = losses / (counts * float(4 * quarter * quarter))

    outward.wait_send()
    pass_near.wait_send()

    @pl.when(core == 0)
    def _():
        to_relay.wait_send()
        pass_far.wait_send()
        core_copy(0).wait_send()

    @pl.when(core == 1)
    def _():
        to_sibling.wait_send()
        far_part.wait_send()

    core_copy(1).wait_send()
    near_part.wait_send()
    for part in range(len(SUM_PARTS)):
        for way in (0, 1):
            hop_copy(part, way).wait_send()
            near_copy(part, way).wait_send()
            far_copy(part, way).wait_send()
    all_sent = row_send.at[:, pl.ds(0, PLANE - 1)]
    pltpu.make_async_copy(all_sent, all_sent, plane_sent).wait()
    pltpu.make_async_copy(all_rows, all_rows, row_sent).wait()


def shards(images, texts, log_scale, bias, block_mask, data_order):
    rows_group, width = images.shape
    quarter = texts.shape[0]
    words = 5 * LANES
    n_z = quarter // PLANE
    parts = len(SUM_PARTS)
    vmem = pl.BlockSpec(memory_space=pltpu.VMEM)
    smem = pl.BlockSpec(memory_space=pltpu.SMEM)
    hbm = pl.BlockSpec(memory_space=pl.ANY)
    dma = pltpu.SemaphoreType.DMA
    image_grad, text_grad, pair_loss = pl.pallas_call(
        kernel,
        out_shape=(
            jax.ShapeDtypeStruct((quarter, width), jnp.float32),
            jax.ShapeDtypeStruct((quarter, width), jnp.float32),
            jax.ShapeDtypeStruct((1, 1), jnp.float32),
        ),
        in_specs=[hbm, hbm, smem, smem, smem, hbm],
        out_specs=(vmem, vmem, vmem),
        scratch_shapes=[
            pltpu.VMEM((rows_group, width), jnp.bfloat16),
            pltpu.VMEM((quarter, width), jnp.bfloat16),
            pltpu.VMEM((1, quarter), jnp.int32),
            pltpu.VMEM((rows_group, width), jnp.bfloat16),
            pltpu.VMEM((rows_group, 1), jnp.float32),
            pltpu.VMEM((5, quarter, width), jnp.bfloat16),
            pltpu.VMEM((rows_group, 4 * quarter), jnp.bfloat16),
            pltpu.VMEM((rows_group, quarter), jnp.float32),
            pltpu.VMEM((quarter, quarter), jnp.float32),
            pltpu.VMEM((quarter, width), jnp.float32),
            pltpu.VMEM((quarter, width), jnp.float32),
            pltpu.VMEM((2, quarter, width), jnp.float32),
            pltpu.VMEM((2, quarter, width), jnp.float32),
            pltpu.VMEM((2, quarter, words), jnp.int32),
            pltpu.VMEM((2, quarter, words), jnp.int32),
            pltpu.VMEM((3, quarter, words), jnp.int32),
            pltpu.VMEM((3, quarter, words), jnp.int32),
            pltpu.VMEM((2, quarter // 2, words), jnp.int32),
            pltpu.VMEM((5, PLANE, n_z, LANES), jnp.int32),
            pltpu.VMEM((5, PLANE, n_z, LANES), jnp.int32),
            pltpu.VMEM((5, PLANE, n_z, LANES), jnp.int32),
            dma((3,)),
            dma((4,)),
            dma((5,)),
            dma((2,)),
            dma((2,)),
            dma((2,)),
            dma((2,)),
            dma((parts, 2)),
            dma((parts, 2)),
            dma((parts, 2)),
            dma((parts, 2)),
            dma((parts, 2)),
            dma((parts, 2)),
            dma,
            dma((parts,)),
            dma,
            dma,
            dma,
        ],
        compiler_params=pltpu.CompilerParams(
            collective_id=0, has_side_effects=True, vmem_limit_bytes=64 * 1024 * 1024
        ),
    )(
        images,
        texts,
        log_scale.reshape(1),
        bias.reshape(1),
        block_mask,
        data_order.reshape(1, quarter),
    )
    return image_grad, text_grad, pair_loss.reshape(())


def solution(mesh):
    in_specs = (
        P("batch", None),
        P(("batch", "tower"), None),
        P(),
        P(),
        P("batch", None),
        P(("batch", "tower")),
    )
    out_specs = (P(("batch", "tower"), None), P(("batch", "tower"), None), P())
    return jax.shard_map(shards, mesh=mesh, in_specs=in_specs, out_specs=out_specs, check_vma=False)
```

```python
import functools

import jax
import jax.numpy as jnp
from jax import lax
from jax.experimental import pallas as pl
from jax.experimental.pallas import tpu as pltpu
from jax.sharding import PartitionSpec as P

NORM_EPS = 1e-06
MESH = pl.DeviceIdType.MESH
LANES = 128
TOP = 32760.0
LOG_STEP = 0.6931471805599453 / 256.0
NT = (((1,), (1,)), ((), ()))
TN = (((0,), (0,)), ((), ()))
NN = (((1,), (0,)), ((), ()))


def mxu(a, b, dims):
    return lax.dot_general(a, b, dims, preferred_element_type=jnp.float32)


def row_inv(wide):
    return lax.rsqrt(jnp.sum(wide * wide, axis=-1, keepdims=True) + NORM_EPS)


def as_codes(rows):
    top = jnp.maximum(jnp.max(jnp.abs(rows), axis=-1, keepdims=True), 1e-30)
    power = jnp.ceil(jnp.log(top) * (1.0 / LOG_STEP))
    codes = jnp.round(rows * (TOP * jnp.exp(power * -LOG_STEP))).astype(jnp.int32)
    return codes, power.astype(jnp.int32)


def step_of(power):
    return jnp.exp(power.astype(jnp.float32) * LOG_STEP) * (1.0 / TOP)


def lane_ids(rows):
    return lax.broadcasted_iota(jnp.int32, (rows, LANES), 1)


def words_of(codes, extras):
    group = [codes[:, LANES * k : LANES * (k + 1)] for k in range(9)]
    pairs = [(group[8], extras)] + [(group[k], group[k + 4]) for k in range(4)]
    return [word_of(high, low) for high, low in pairs]


def word_of(high, low):
    return (high << 16) | (low & 0xFFFF)


def high_of(word):
    return word >> 16


def low_of(word):
    return (word << 16) >> 16


def loss_fields(total):
    power = jnp.ceil(jnp.log(jnp.maximum(total, 1e-30)) * (1.0 / 0.6931471805599453))
    scaled = total * jnp.exp(power * -0.6931471805599453) * 8192.0
    first = jnp.floor(scaled)
    second = jnp.floor((scaled - first) * 16384.0)
    return [v.astype(jnp.int32) for v in (power, first, second)]


def loss_from(power, first, second):
    wide = first.astype(jnp.float32) + second.astype(jnp.float32) * (1.0 / 16384.0)
    return wide * jnp.exp(power.astype(jnp.float32) * 0.6931471805599453) * (1.0 / 8192.0)


PLANE = 8
SUM_PARTS = ((0, 3), (3, 5))
ROW_PARTS = ((0, 2), (2, 5))
PIECES = 2


def kernel(
    images_hbm,
    texts_hbm,
    log_scale_ref,
    bias_ref,
    mask_ref,
    order_hbm,
    image_grad_ref,
    text_grad_ref,
    loss_ref,
    images_ref,
    texts_ref,
    order_ref,
    img_unit,
    img_inv,
    cand,
    coeffs,
    dots,
    loss_acc,
    own_text,
    own_image,
    core_send,
    core_recv,
    part_send,
    part_recv,
    tower_send,
    tower_recv,
    hop_send,
    hop_recv,
    kept,
    row_send,
    row_mid,
    row_recv,
    in_here,
    cand_sent,
    cand_here,
    core_sent,
    core_here,
    part_sent,
    part_here,
    hop_sent,
    hop_here,
    block_sent,
    block_here,
    plane_sent,
    plane_here,
    row_sent,
    row_here,
    row_own,
):
    n_batch = lax.axis_size("batch")
    n_tower = lax.axis_size("tower")
    n_z = n_batch // PLANE
    me = lax.axis_index("batch")
    tower = lax.axis_index("tower")
    z = me // PLANE
    j = lax.rem(me, PLANE)
    core = lax.rem(me, 2)
    sibling = me + 1 - 2 * core
    quarter, width = texts_ref.shape
    half = quarter // 2

    def batch_at(offset):
        return lax.rem(me + (n_batch + offset), n_batch)

    def tower_at(offset):
        return lax.rem(tower + offset, n_tower)

    def z_step(i):
        return n_z // 2 + ((i + 1) // 2) * (1 - 2 * lax.rem(i, 2))

    def column_at(i):
        return lax.rem(z + z_step(i), n_z) * PLANE + j

    def remote(source, target, sent, here, dest):
        return pltpu.make_async_remote_copy(
            src_ref=source,
            dst_ref=target,
            send_sem=sent,
            recv_sem=here,
            device_id=dest,
            device_id_type=MESH,
        )

    loads = [
        pltpu.make_async_copy(texts_hbm, texts_ref, in_here.at[0]),
        pltpu.make_async_copy(images_hbm, images_ref, in_here.at[1]),
        pltpu.make_async_copy(order_hbm, order_ref, in_here.at[2]),
    ]
    for load in loads:
        load.start()

    chips = n_batch // 2
    relay_to = z * PLANE + lax.rem(j + 2, PLANE)
    relayed = lax.rem(z * (PLANE // 2) + lax.rem(j // 2 + 3, PLANE // 2) + chips - 2, chips) * 2 + 1
    chip_after = lax.rem(me // 2 + 2, chips)
    relay_from = ((chip_after // 4) * 4 + lax.rem(lax.rem(chip_after, 4) + 1, 4)) * 2

    barrier = pltpu.get_barrier_semaphore()

    def greet(dest):
        pl.semaphore_signal(barrier, 1, device_id=dest, device_id_type=MESH)

    def greet_column(i, _):
        greet({"batch": column_at(i)})
        return 0

    def greet_plane(i, _):
        greet({"batch": z * PLANE + lax.rem(j + i, PLANE)})
        return 0

    lax.fori_loop(0, n_z - 1, greet_column, 0)
    greet({"tower": tower_at(1)})
    greet({"tower": tower_at(n_tower - 1)})

    @pl.when(core == 0)
    def _():
        greet({"batch": batch_at(3)})
        greet({"batch": batch_at(-1)})

    @pl.when(core == 1)
    def _():
        greet({"batch": relay_from})
        for d in (-3, 1, 2, -2):
            greet({"batch": batch_at(d)})

    lax.fori_loop(1, PLANE, greet_plane, 0)

    loads[0].wait()
    wide = texts_ref[...].astype(jnp.float32)
    cand[0] = (wide * row_inv(wide)).astype(jnp.bfloat16)

    pl.semaphore_wait(barrier, n_z - 1 + PLANE - 1 + 2 + 3 + core)

    piece = quarter // PIECES

    def cand_copy(source, target, dest, sem, n):
        rows = pl.ds(n * piece, piece)
        return remote(
            cand.at[source, rows],
            cand.at[target, rows],
            cand_sent.at[sem, n],
            cand_here.at[target, n],
            {"batch": dest},
        )

    def outward(n):
        return cand_copy(0, 1 + 2 * core, batch_at(-1 - 2 * core), 0, n)

    def to_sibling(n):
        return cand_copy(0, 1, sibling, 1, n)

    def to_relay(n):
        return cand_copy(0, 4, relay_to, 1, n)

    def pass_far(n):
        return cand_copy(4, 3, relayed, 2, n)

    def pass_near(n):
        return cand_copy(3 - 2 * core, 2, sibling, 3, n)

    def text_here(slot, n):
        cand_copy(0, slot, me, 0, n).wait_recv()

    for n in range(PIECES):

        @pl.when(core == 0)
        def _():
            to_relay(n).start()

        outward(n).start()

    @pl.when(core == 1)
    def _():
        for n in range(PIECES):
            to_sibling(n).start()

    loads[1].wait()

    def norm(q, _):
        rows = pl.ds(q * quarter, quarter)
        values = images_ref[rows, :].astype(jnp.float32)
        inv = row_inv(values)
        img_inv[rows, :] = inv
        img_unit[rows, :] = (values * inv).astype(jnp.bfloat16)
        return 0

    lax.fori_loop(0, n_tower, norm, 0)

    logit_scale = jnp.exp(jnp.full((1, LANES), log_scale_ref[0], jnp.float32))
    bias = bias_ref[0]
    loss_acc[...] = jnp.zeros_like(loss_acc)
    diagonal = lax.broadcasted_iota(jnp.int32, (quarter, quarter), 0) == lax.broadcasted_iota(
        jnp.int32, (quarter, quarter), 1
    )

    def pairs(k, own):
        dots[...] = mxu(img_unit[...], cand[k], NT)

        def some(q, _):
            rows = pl.ds(pl.multiple_of(q * quarter, quarter), quarter)
            logits = logit_scale * dots[rows, :] + bias
            small = jnp.exp(-jnp.abs(logits))
            share = 1.0 / (1.0 + small)
            sigmoid = jnp.where(logits >= 0.0, share, small * share)
            loss = jnp.maximum(logits, 0.0) + jnp.log1p(small)
            chosen = mask_ref[q // 2, 2 * k + tower // 2].astype(jnp.float32)
            if own:
                positive = jnp.where(diagonal & (q == tower), 1.0, 0.0)
                loss = loss - positive * logits
                sigmoid = sigmoid - positive
            loss_acc[...] += chosen * loss
            cols = pl.ds(pl.multiple_of(k * quarter, quarter), quarter)
            coeffs[rows, cols] = (chosen * logit_scale * sigmoid).astype(jnp.bfloat16)
            return 0

        lax.fori_loop(0, n_tower, some, 0)

    def text_part(k):
        cols = pl.ds(pl.multiple_of(k * quarter, quarter), quarter)
        return mxu(coeffs[:, cols], img_unit[...], TN)

    def fields(values, rows):
        out = jnp.zeros((rows, LANES), jnp.int32)
        for n, value in enumerate(values):
            out = jnp.where(lane_ids(rows) == n, value, out)
        return out

    def put_rows(ref, rows, more):
        codes, power = as_codes(rows)
        for n, word in enumerate(words_of(codes, fields([power, *more], rows.shape[0]))):
            ref[:, LANES * n : LANES * (n + 1)] = word

    def get_rows(ref):
        words = [ref[:, LANES * n : LANES * (n + 1)] for n in range(5)]
        codes = [high_of(w) for w in words[1:]] + [low_of(w) for w in words[1:]] + [high_of(words[0])]
        step = step_of(low_of(words[0])[:, 0:1])
        return jnp.concatenate(codes, axis=1).astype(jnp.float32) * step

    pairs(0, True)
    own_text[...] = text_part(0)

    @pl.when(core == 0)
    def _():
        for n in range(PIECES):
            text_here(4, n)
            pass_far(n).start()

    for n in range(PIECES):
        text_here(1, n)

        @pl.when(core == 1)
        def _():
            pass_near(n).start()

    pairs(1, False)

    def core_copy(n):
        return remote(
            core_send.at[n], core_recv.at[n], core_sent.at[n], core_here.at[n], {"batch": sibling}
        )

    @pl.when(core == 0)
    def _():
        core_send[0] = text_part(1)
        core_copy(0).start()

    second_slot = 3 - core
    third_slot = 2 + core
    for n in range(PIECES):
        text_here(second_slot, n)

        @pl.when(core == 0)
        def _():
            pass_near(n).start()

    pairs(second_slot, False)

    @pl.when(core == 1)
    def _():
        core_send[1] = text_part(2)
        core_copy(1).start()

    for n in range(PIECES):
        text_here(third_slot, n)
    pairs(third_slot, False)

    def part_copy(n, dest):
        return remote(
            part_send.at[n], part_recv.at[n], part_sent.at[n], part_here.at[n], {"batch": dest}
        )

    far_part = part_copy(0, batch_at(2))
    near_part = part_copy(1, batch_at(3 - 2 * core))

    def text_sums(which):
        @pl.when(core == which)
        def _():
            core_copy(1).wait_recv()
            rest = text_part(3 - 2 * which) + core_recv[1]
            if which == 1:
                far_part.wait_recv()
                rest = rest + get_rows(part_recv.at[0])
            put_rows(part_send.at[1], rest, [])
            near_part.start()

    total = jnp.sum(jnp.sum(loss_acc[...], axis=1, keepdims=True), axis=0, keepdims=True)

    def image_part(q):
        rows = pl.ds(pl.multiple_of(q * quarter, quarter), quarter)
        texts = cand[0:4].reshape(4 * quarter, width)
        back = mxu(coeffs[rows, :], texts, NN)
        inv = img_inv[rows, :]
        unit = images_ref[rows, :].astype(jnp.float32) * inv
        return (back - unit * jnp.sum(unit * back, axis=-1, keepdims=True)) * inv

    def cut(part):
        first, last = SUM_PARTS[part]
        return pl.ds(first * LANES, (last - first) * LANES)

    def hop_copy(way):
        return remote(
            hop_send.at[pl.ds(way * half, half)],
            hop_recv.at[way],
            hop_sent.at[way],
            hop_here.at[way],
            {"tower": tower_at(1 + 2 * way)},
        )

    def block_copy(part, way, summed):
        rows = pl.ds((way if summed else 1 - way) * half, half)
        return remote(
            tower_send.at[way, rows, cut(part)],
            tower_recv.at[way, rows, cut(part)],
            block_sent.at[part, way, summed],
            block_here.at[part, way, summed],
            {"tower": tower_at(1 + 2 * way)},
        )

    put_rows(hop_send, image_part(tower_at(2)), loss_fields(total))
    for way in (0, 1):
        hop_copy(way).start()

    @pl.when(core == 1)
    def _():
        put_rows(part_send.at[0], text_part(3), [])
        far_part.start()

    @pl.when(core == 0)
    def _():
        core_send[1] = text_part(2)
        core_copy(1).start()

    text_sums(0)

    for way in (0, 1):
        block = image_part(tower_at(1 + 2 * way))
        kept[way] = block[way * half : (way + 1) * half]
        direct = block[(1 - way) * half : (2 - way) * half]
        put_rows(tower_send.at[way, pl.ds((1 - way) * half, half)], direct, loss_fields(total))
        block_copy(0, way, 0).start()

    own_image[...] = image_part(tower)

    order = order_ref
    loads[2].wait()
    place = lax.broadcasted_iota(jnp.int32, (quarter, quarter), 0)
    goal = lax.rem(z + z_step(lax.rem(place, n_z)), n_z) * PLANE + place // n_z
    picks = goal == order[...] // (n_tower * quarter)
    slots = jnp.sum(jnp.where(picks, lax.rem(order[...], quarter), 0), axis=1, keepdims=True)
    one_hot = jnp.where(picks, 1.0, 0.0).astype(jnp.bfloat16)

    def bytes_of(whole):
        return whole.astype(jnp.float32).astype(jnp.bfloat16)

    def moved(matrix, whole, dims):
        high, low = bytes_of(whole >> 8), bytes_of(whole & 0xFF)
        return mxu(matrix, high, dims) * 256.0 + mxu(matrix, low, dims)

    count = mask_ref[0, 0] * 0
    for p in range(mask_ref.shape[0]):
        for c in range(mask_ref.shape[1]):
            count = count + mask_ref[p, c]

    def plane_copy(part, peer):
        first, last = ROW_PARTS[part]
        return remote(
            row_send.at[pl.ds(first, last - first), peer],
            row_mid.at[pl.ds(first, last - first), j],
            plane_sent,
            plane_here.at[part],
            {"batch": z * PLANE + peer},
        )

    def column_copy(part, i):
        first, last = ROW_PARTS[part]
        here = row_mid.at[pl.ds(first, last - first), :, pl.ds(i, 1), :]
        there = row_recv.at[pl.ds(first, last - first), :, pl.ds(i, 1), :]
        return remote(here, there, row_sent, row_here, {"batch": column_at(i)})

    def to_plane(part):
        first, last = ROW_PARTS[part]

        def some(i, _):
            plane_copy(part, lax.rem(j + i, PLANE)).start()
            return 0

        lax.fori_loop(1, PLANE, some, 0)
        for n in range(first, last):
            row_mid[n, pl.ds(j, 1)] = row_send[n, pl.ds(j, 1)]

    def to_column(part):
        first, last = ROW_PARTS[part]
        others = row_mid.at[pl.ds(first, last - first), pl.ds(0, PLANE - 1)]
        pltpu.make_async_copy(others, others, plane_here.at[part]).wait()

        def some(i, _):
            column_copy(part, i).start()
            return 0

        lax.fori_loop(0, n_z - 1, some, 0)

    def pass_on():
        for way in (0, 1):
            hop_copy(way).wait_recv()
            extras = low_of(hop_recv[way, 0:8, 0:LANES])
            both = total + loss_from(extras[0:1, 1:2], extras[0:1, 2:3], extras[0:1, 3:4])
            rows = kept[way] + get_rows(hop_recv.at[way])
            put_rows(tower_send.at[way, pl.ds(way * half, half)], rows, loss_fields(both))
            block_copy(0, way, 1).start()
        for part in range(1, len(SUM_PARTS)):
            for way in (0, 1):
                block_copy(part, way, 0).start()
                block_copy(part, way, 1).start()

    powers = []
    steps = []
    spare = None
    for part, (first, last) in enumerate(SUM_PARTS):
        if part == 0:
            pass_on()
        for way in (0, 1):
            for summed in (0, 1):
                block_copy(part, way, summed).wait_recv()
        if part == 0:
            for n in range(2):
                extras = low_of(tower_recv[n, :, 0:LANES])
                steps.append(step_of(extras[:, 0:1]))
                total = total + loss_from(extras[0:1, 1:2], extras[0:1, 2:3], extras[0:1, 3:4])
            spare = own_image[:, 8 * LANES :]
            for n in range(2):
                spare = spare + high_of(tower_recv[n, :, 0:LANES]).astype(jnp.float32) * steps[n]
        rows = []
        for group in range(max(first, 1), last):
            high = own_image[:, (group - 1) * LANES : group * LANES]
            low = own_image[:, (group + 3) * LANES : (group + 4) * LANES]
            for n in range(2):
                word = tower_recv[n, :, group * LANES : (group + 1) * LANES]
                high = high + high_of(word).astype(jnp.float32) * steps[n]
                low = low + low_of(word).astype(jnp.float32) * steps[n]
            rows += [high, low]
        final = part == len(SUM_PARTS) - 1
        if final:
            rows.append(spare)
        codes, power = as_codes(jnp.concatenate(rows, axis=1))
        powers.append(power)
        if final:
            codes = jnp.concatenate([codes, fields(powers, quarter)], axis=1)
        codes = moved(one_hot, codes, NN).astype(jnp.int32)
        groups = [codes[:, LANES * n : LANES * (n + 1)] for n in range(codes.shape[1] // LANES)]
        if final:
            for n, value in enumerate([slots, count, *loss_fields(total)]):
                groups[-1] = jnp.where(lane_ids(quarter) == len(powers) + n, value, groups[-1])
        for n in range(len(groups) // 2):
            word = word_of(groups[2 * n], groups[2 * n + 1])
            row_send[ROW_PARTS[part][0] + n] = word.reshape(PLANE, n_z, LANES)
        to_plane(part)
        if part == 0:
            text_sums(1)
        to_column(part)

    own_here = row_mid.at[:, :, pl.ds(n_z - 1, 1), :]
    own_there = row_recv.at[:, :, pl.ds(n_z - 1, 1), :]
    own_copy = pltpu.make_async_copy(own_here, own_there, row_own)
    own_copy.start()

    near_part.wait_recv()
    own_text[...] += get_rows(part_recv.at[1])

    @pl.when(core == 1)
    def _():
        core_copy(0).wait_recv()
        own_text[...] += core_recv[0]

    back = own_text[...]
    wide = texts_ref[...].astype(jnp.float32)
    inv = row_inv(wide)
    unit = wide * inv
    text_grad_ref[...] = (back - unit * jnp.sum(unit * back, axis=-1, keepdims=True)) * inv

    own_copy.wait()
    all_rows = row_recv.at[:, :, pl.ds(0, n_z - 1), :]
    pltpu.make_async_copy(all_rows, all_rows, row_here).wait()
    words = [row_recv[n].reshape(quarter, LANES) for n in range(5)]
    extras = low_of(words[4])
    n_powers = len(powers)
    places = jnp.where(lane_ids(quarter) == extras[:, n_powers : n_powers + 1], 1.0, 0.0)
    places = places.astype(jnp.bfloat16)
    sizes = jnp.exp(moved(places, extras, TN) * LOG_STEP) * (1.0 / TOP)

    def put_group(group, whole, part):
        image_grad_ref[:, LANES * group : LANES * (group + 1)] = (
            moved(places, whole, TN) * sizes[:, part : part + 1]
        )

    for part, (first, last) in enumerate(ROW_PARTS):
        for n in range(first, min(last, 4)):
            put_group(n, high_of(words[n]), part)
            put_group(n + 4, low_of(words[n]), part)
    put_group(8, high_of(words[4]), len(ROW_PARTS) - 1)
    tail = [extras[:, n_powers + n : n_powers + n + 1] for n in range(1, 5)]
    losses = jnp.sum(loss_from(*tail[1:]), axis=0, keepdims=True)
    counts = jnp.sum(tail[0].astype(jnp.float32), axis=0, keepdims=True)
    loss_ref[...] = losses / (counts * float(4 * quarter * quarter))

    for n in range(PIECES):
        outward(n).wait_send()
        pass_near(n).wait_send()

    @pl.when(core == 0)
    def _():
        for n in range(PIECES):
            to_relay(n).wait_send()
            pass_far(n).wait_send()
        core_copy(0).wait_send()

    @pl.when(core == 1)
    def _():
        for n in range(PIECES):
            to_sibling(n).wait_send()
        far_part.wait_send()

    core_copy(1).wait_send()
    near_part.wait_send()
    for way in (0, 1):
        hop_copy(way).wait_send()
        for part in range(len(SUM_PARTS)):
            for summed in (0, 1):
                block_copy(part, way, summed).wait_send()
    all_sent = row_send.at[:, pl.ds(0, PLANE - 1)]
    pltpu.make_async_copy(all_sent, all_sent, plane_sent).wait()
    pltpu.make_async_copy(all_rows, all_rows, row_sent).wait()


def hand_out(image_in, text_in, image_out, text_out, held, done):
    ins = [
        pltpu.make_async_copy(image_in, held.at[0], done.at[0]),
        pltpu.make_async_copy(text_in, held.at[1], done.at[1]),
    ]
    outs = [
        pltpu.make_async_copy(held.at[0], image_out, done.at[2]),
        pltpu.make_async_copy(held.at[1], text_out, done.at[3]),
    ]
    for copy in ins:
        copy.start()
    for n in range(2):
        ins[n].wait()
        outs[n].start()
    for copy in outs:
        copy.wait()


def shards(images, texts, log_scale, bias, block_mask, data_order):
    rows_group, width = images.shape
    quarter = texts.shape[0]
    words = 5 * LANES
    n_z = quarter // PLANE
    parts = len(SUM_PARTS)
    vmem = pl.BlockSpec(memory_space=pltpu.VMEM)
    smem = pl.BlockSpec(memory_space=pltpu.SMEM)
    hbm = pl.BlockSpec(memory_space=pl.ANY)
    dma = pltpu.SemaphoreType.DMA
    image_grad, text_grad, pair_loss = pl.pallas_call(
        kernel,
        out_shape=(
            jax.ShapeDtypeStruct((quarter, width), jnp.float32),
            jax.ShapeDtypeStruct((quarter, width), jnp.float32),
            jax.ShapeDtypeStruct((1, 1), jnp.float32),
        ),
        in_specs=[hbm, hbm, smem, smem, smem, hbm],
        out_specs=(vmem, vmem, vmem),
        scratch_shapes=[
            pltpu.VMEM((rows_group, width), jnp.bfloat16),
            pltpu.VMEM((quarter, width), jnp.bfloat16),
            pltpu.VMEM((1, quarter), jnp.int32),
            pltpu.VMEM((rows_group, width), jnp.bfloat16),
            pltpu.VMEM((rows_group, 1), jnp.float32),
            pltpu.VMEM((5, quarter, width), jnp.bfloat16),
            pltpu.VMEM((rows_group, 4 * quarter), jnp.bfloat16),
            pltpu.VMEM((rows_group, quarter), jnp.float32),
            pltpu.VMEM((quarter, quarter), jnp.float32),
            pltpu.VMEM((quarter, width), jnp.float32),
            pltpu.VMEM((quarter, width), jnp.float32),
            pltpu.VMEM((2, quarter, width), jnp.float32),
            pltpu.VMEM((2, quarter, width), jnp.float32),
            pltpu.VMEM((2, quarter, words), jnp.int32),
            pltpu.VMEM((2, quarter, words), jnp.int32),
            pltpu.VMEM((2, quarter, words), jnp.int32),
            pltpu.VMEM((2, quarter, words), jnp.int32),
            pltpu.VMEM((quarter, words), jnp.int32),
            pltpu.VMEM((2, quarter // 2, words), jnp.int32),
            pltpu.VMEM((2, quarter // 2, width), jnp.float32),
            pltpu.VMEM((5, PLANE, n_z, LANES), jnp.int32),
            pltpu.VMEM((5, PLANE, n_z, LANES), jnp.int32),
            pltpu.VMEM((5, PLANE, n_z, LANES), jnp.int32),
            dma((3,)),
            dma((4, PIECES)),
            dma((5, PIECES)),
            dma((2,)),
            dma((2,)),
            dma((2,)),
            dma((2,)),
            dma((2,)),
            dma((2,)),
            dma((parts, 2, 2)),
            dma((parts, 2, 2)),
            dma,
            dma((parts,)),
            dma,
            dma,
            dma,
        ],
        compiler_params=pltpu.CompilerParams(
            collective_id=0, has_side_effects=True, vmem_limit_bytes=64 * 1024 * 1024
        ),
    )(
        images,
        texts,
        log_scale.reshape(1),
        bias.reshape(1),
        block_mask,
        data_order.reshape(1, quarter),
    )
    image_grad, text_grad = pl.pallas_call(
        hand_out,
        out_shape=(
            jax.ShapeDtypeStruct((quarter, width), jnp.float32),
            jax.ShapeDtypeStruct((quarter, width), jnp.float32),
        ),
        in_specs=[pl.BlockSpec(memory_space=pltpu.HBM)] * 2,
        out_specs=(pl.BlockSpec(memory_space=pltpu.HBM),) * 2,
        scratch_shapes=[pltpu.VMEM((2, quarter, width), jnp.float32), dma((4,))],
    )(image_grad, text_grad)
    return image_grad, text_grad, pair_loss.reshape(())


def solution(mesh):
    in_specs = (
        P("batch", None),
        P(("batch", "tower"), None),
        P(),
        P(),
        P("batch", None),
        P(("batch", "tower")),
    )
    out_specs = (P(("batch", "tower"), None), P(("batch", "tower"), None), P())
    return jax.shard_map(shards, mesh=mesh, in_specs=in_specs, out_specs=out_specs, check_vma=False)
```

```python
import functools

import jax
import jax.numpy as jnp
from jax import lax
from jax.experimental import pallas as pl
from jax.experimental.pallas import tpu as pltpu
from jax.sharding import PartitionSpec as P

NORM_EPS = 1e-06
MESH = pl.DeviceIdType.MESH
LANES = 128
TOP = 32760.0
LOG_STEP = 0.6931471805599453 / 256.0
NT = (((1,), (1,)), ((), ()))
TN = (((0,), (0,)), ((), ()))
NN = (((1,), (0,)), ((), ()))


def mxu(a, b, dims):
    return lax.dot_general(a, b, dims, preferred_element_type=jnp.float32)


def row_inv(wide):
    return lax.rsqrt(jnp.sum(wide * wide, axis=-1, keepdims=True) + NORM_EPS)


def as_codes(rows):
    top = jnp.maximum(jnp.max(jnp.abs(rows), axis=-1, keepdims=True), 1e-30)
    power = jnp.ceil(jnp.log(top) * (1.0 / LOG_STEP))
    codes = jnp.round(rows * (TOP * jnp.exp(power * -LOG_STEP))).astype(jnp.int32)
    return codes, power.astype(jnp.int32)


def step_of(power):
    return jnp.exp(power.astype(jnp.float32) * LOG_STEP) * (1.0 / TOP)


def lane_ids(rows):
    return lax.broadcasted_iota(jnp.int32, (rows, LANES), 1)


def words_of(codes, extras):
    group = [codes[:, LANES * k : LANES * (k + 1)] for k in range(9)]
    pairs = [(group[8], extras)] + [(group[k], group[k + 4]) for k in range(4)]
    return [word_of(high, low) for high, low in pairs]


def word_of(high, low):
    return (high << 16) | (low & 0xFFFF)


def high_of(word):
    return word >> 16


def low_of(word):
    return (word << 16) >> 16


def bytes_of(whole):
    return whole.astype(jnp.float32).astype(jnp.bfloat16)


def moved(matrix, whole, dims):
    high, low = bytes_of(whole >> 8), bytes_of(whole & 0xFF)
    return mxu(matrix, high, dims) * 256.0 + mxu(matrix, low, dims)


def loss_fields(total):
    power = jnp.ceil(jnp.log(jnp.maximum(total, 1e-30)) * (1.0 / 0.6931471805599453))
    scaled = total * jnp.exp(power * -0.6931471805599453) * 8192.0
    first = jnp.floor(scaled)
    second = jnp.floor((scaled - first) * 16384.0)
    return [v.astype(jnp.int32) for v in (power, first, second)]


def loss_from(power, first, second):
    wide = first.astype(jnp.float32) + second.astype(jnp.float32) * (1.0 / 16384.0)
    return wide * jnp.exp(power.astype(jnp.float32) * 0.6931471805599453) * (1.0 / 8192.0)


PLANE = 8
SUM_PARTS = ((0, 3), (3, 5))
ROW_PARTS = ((0, 2), (2, 5))
PIECES = 2


def kernel(
    images_hbm,
    texts_hbm,
    log_scale_ref,
    bias_ref,
    mask_ref,
    order_hbm,
    words_hbm,
    text_hbm,
    loss_ref,
    images_ref,
    texts_ref,
    order_ref,
    img_unit,
    img_inv,
    cand,
    coeffs,
    dots,
    loss_acc,
    own_text,
    own_image,
    core_send,
    core_recv,
    part_send,
    part_recv,
    tower_send,
    tower_recv,
    hop_send,
    hop_recv,
    kept,
    row_send,
    row_mid,
    row_recv,
    in_here,
    cand_sent,
    cand_here,
    core_sent,
    core_here,
    part_sent,
    part_here,
    hop_sent,
    hop_here,
    block_sent,
    block_here,
    plane_sent,
    plane_here,
    row_sent,
    row_here,
    row_own,
    text_grad_ref,
    out_here,
):
    n_batch = lax.axis_size("batch")
    n_tower = lax.axis_size("tower")
    n_z = n_batch // PLANE
    me = lax.axis_index("batch")
    tower = lax.axis_index("tower")
    z = me // PLANE
    j = lax.rem(me, PLANE)
    core = lax.rem(me, 2)
    sibling = me + 1 - 2 * core
    quarter, width = texts_ref.shape
    half = quarter // 2

    def batch_at(offset):
        return lax.rem(me + (n_batch + offset), n_batch)

    def tower_at(offset):
        return lax.rem(tower + offset, n_tower)

    def z_step(i):
        return n_z // 2 + ((i + 1) // 2) * (1 - 2 * lax.rem(i, 2))

    def column_at(i):
        return lax.rem(z + z_step(i), n_z) * PLANE + j

    def remote(source, target, sent, here, dest):
        return pltpu.make_async_remote_copy(
            src_ref=source,
            dst_ref=target,
            send_sem=sent,
            recv_sem=here,
            device_id=dest,
            device_id_type=MESH,
        )

    loads = [
        pltpu.make_async_copy(texts_hbm, texts_ref, in_here.at[0]),
        pltpu.make_async_copy(images_hbm, images_ref, in_here.at[1]),
        pltpu.make_async_copy(order_hbm, order_ref, in_here.at[2]),
    ]
    for load in loads:
        load.start()

    chips = n_batch // 2
    relay_to = z * PLANE + lax.rem(j + 2, PLANE)
    relayed = lax.rem(z * (PLANE // 2) + lax.rem(j // 2 + 3, PLANE // 2) + chips - 2, chips) * 2 + 1
    chip_after = lax.rem(me // 2 + 2, chips)
    relay_from = ((chip_after // 4) * 4 + lax.rem(lax.rem(chip_after, 4) + 1, 4)) * 2

    barrier = pltpu.get_barrier_semaphore()

    def greet(dest):
        pl.semaphore_signal(barrier, 1, device_id=dest, device_id_type=MESH)

    def greet_column(i, _):
        greet({"batch": column_at(i)})
        return 0

    def greet_plane(i, _):
        greet({"batch": z * PLANE + lax.rem(j + i, PLANE)})
        return 0

    lax.fori_loop(0, n_z - 1, greet_column, 0)
    greet({"tower": tower_at(1)})
    greet({"tower": tower_at(n_tower - 1)})

    @pl.when(core == 0)
    def _():
        greet({"batch": batch_at(3)})
        greet({"batch": batch_at(-1)})

    @pl.when(core == 1)
    def _():
        greet({"batch": relay_from})
        for d in (-3, 1, 2, -2):
            greet({"batch": batch_at(d)})

    lax.fori_loop(1, PLANE, greet_plane, 0)

    loads[0].wait()
    wide = texts_ref[...].astype(jnp.float32)
    cand[0] = (wide * row_inv(wide)).astype(jnp.bfloat16)

    pl.semaphore_wait(barrier, n_z - 1 + PLANE - 1 + 2 + 3 + core)

    piece = quarter // PIECES

    def cand_copy(source, target, dest, sem, n):
        rows = pl.ds(n * piece, piece)
        return remote(
            cand.at[source, rows],
            cand.at[target, rows],
            cand_sent.at[sem, n],
            cand_here.at[target, n],
            {"batch": dest},
        )

    def outward(n):
        return cand_copy(0, 1 + 2 * core, batch_at(-1 - 2 * core), 0, n)

    def to_sibling(n):
        return cand_copy(0, 1, sibling, 1, n)

    def to_relay(n):
        return cand_copy(0, 4, relay_to, 1, n)

    def pass_far(n):
        return cand_copy(4, 3, relayed, 2, n)

    def pass_near(n):
        return cand_copy(3 - 2 * core, 2, sibling, 3, n)

    def text_here(slot, n):
        cand_copy(0, slot, me, 0, n).wait_recv()

    for n in range(PIECES):

        @pl.when(core == 0)
        def _():
            to_relay(n).start()

        outward(n).start()

    @pl.when(core == 1)
    def _():
        for n in range(PIECES):
            to_sibling(n).start()

    loads[1].wait()

    def norm(q, _):
        rows = pl.ds(q * quarter, quarter)
        values = images_ref[rows, :].astype(jnp.float32)
        inv = row_inv(values)
        img_inv[rows, :] = inv
        img_unit[rows, :] = (values * inv).astype(jnp.bfloat16)
        return 0

    lax.fori_loop(0, n_tower, norm, 0)

    logit_scale = jnp.exp(jnp.full((1, LANES), log_scale_ref[0], jnp.float32))
    bias = bias_ref[0]
    loss_acc[...] = jnp.zeros_like(loss_acc)
    diagonal = lax.broadcasted_iota(jnp.int32, (quarter, quarter), 0) == lax.broadcasted_iota(
        jnp.int32, (quarter, quarter), 1
    )

    def pairs(k, own):
        dots[...] = mxu(img_unit[...], cand[k], NT)

        def some(q, _):
            rows = pl.ds(pl.multiple_of(q * quarter, quarter), quarter)
            logits = logit_scale * dots[rows, :] + bias
            small = jnp.exp(-jnp.abs(logits))
            share = 1.0 / (1.0 + small)
            sigmoid = jnp.where(logits >= 0.0, share, small * share)
            loss = jnp.maximum(logits, 0.0) + jnp.log1p(small)
            chosen = mask_ref[q // 2, 2 * k + tower // 2].astype(jnp.float32)
            if own:
                positive = jnp.where(diagonal & (q == tower), 1.0, 0.0)
                loss = loss - positive * logits
                sigmoid = sigmoid - positive
            loss_acc[...] += chosen * loss
            cols = pl.ds(pl.multiple_of(k * quarter, quarter), quarter)
            coeffs[rows, cols] = (chosen * logit_scale * sigmoid).astype(jnp.bfloat16)
            return 0

        lax.fori_loop(0, n_tower, some, 0)

    def text_part(k):
        cols = pl.ds(pl.multiple_of(k * quarter, quarter), quarter)
        return mxu(coeffs[:, cols], img_unit[...], TN)

    def fields(values, rows):
        out = jnp.zeros((rows, LANES), jnp.int32)
        for n, value in enumerate(values):
            out = jnp.where(lane_ids(rows) == n, value, out)
        return out

    def put_rows(ref, rows, more):
        codes, power = as_codes(rows)
        for n, word in enumerate(words_of(codes, fields([power, *more], rows.shape[0]))):
            ref[:, LANES * n : LANES * (n + 1)] = word

    def get_rows(ref):
        words = [ref[:, LANES * n : LANES * (n + 1)] for n in range(5)]
        codes = [high_of(w) for w in words[1:]] + [low_of(w) for w in words[1:]] + [high_of(words[0])]
        step = step_of(low_of(words[0])[:, 0:1])
        return jnp.concatenate(codes, axis=1).astype(jnp.float32) * step

    pairs(0, True)
    own_text[...] = text_part(0)

    @pl.when(core == 0)
    def _():
        for n in range(PIECES):
            text_here(4, n)
            pass_far(n).start()

    for n in range(PIECES):
        text_here(1, n)

        @pl.when(core == 1)
        def _():
            pass_near(n).start()

    pairs(1, False)

    def core_copy(n):
        return remote(
            core_send.at[n], core_recv.at[n], core_sent.at[n], core_here.at[n], {"batch": sibling}
        )

    @pl.when(core == 0)
    def _():
        core_send[0] = text_part(1)
        core_copy(0).start()

    second_slot = 3 - core
    third_slot = 2 + core
    for n in range(PIECES):
        text_here(second_slot, n)

        @pl.when(core == 0)
        def _():
            pass_near(n).start()

    pairs(second_slot, False)

    @pl.when(core == 1)
    def _():
        core_send[1] = text_part(2)
        core_copy(1).start()

    for n in range(PIECES):
        text_here(third_slot, n)
    pairs(third_slot, False)

    def part_copy(n, dest):
        return remote(
            part_send.at[n], part_recv.at[n], part_sent.at[n], part_here.at[n], {"batch": dest}
        )

    far_part = part_copy(0, batch_at(2))
    near_part = part_copy(1, batch_at(3 - 2 * core))

    def text_sums(which):
        @pl.when(core == which)
        def _():
            core_copy(1).wait_recv()
            rest = text_part(3 - 2 * which) + core_recv[1]
            if which == 1:
                far_part.wait_recv()
                rest = rest + get_rows(part_recv.at[0])
            put_rows(part_send.at[1], rest, [])
            near_part.start()

    total = jnp.sum(jnp.sum(loss_acc[...], axis=1, keepdims=True), axis=0, keepdims=True)

    def image_part(q):
        rows = pl.ds(pl.multiple_of(q * quarter, quarter), quarter)
        texts = cand[0:4].reshape(4 * quarter, width)
        back = mxu(coeffs[rows, :], texts, NN)
        inv = img_inv[rows, :]
        unit = images_ref[rows, :].astype(jnp.float32) * inv
        return (back - unit * jnp.sum(unit * back, axis=-1, keepdims=True)) * inv

    def cut(part):
        first, last = SUM_PARTS[part]
        return pl.ds(first * LANES, (last - first) * LANES)

    def hop_copy(way):
        return remote(
            hop_send.at[pl.ds(way * half, half)],
            hop_recv.at[way],
            hop_sent.at[way],
            hop_here.at[way],
            {"tower": tower_at(1 + 2 * way)},
        )

    def block_copy(part, way, summed):
        rows = pl.ds((way if summed else 1 - way) * half, half)
        return remote(
            tower_send.at[way, rows, cut(part)],
            tower_recv.at[way, rows, cut(part)],
            block_sent.at[part, way, summed],
            block_here.at[part, way, summed],
            {"tower": tower_at(1 + 2 * way)},
        )

    put_rows(hop_send, image_part(tower_at(2)), loss_fields(total))
    for way in (0, 1):
        hop_copy(way).start()

    @pl.when(core == 1)
    def _():
        put_rows(part_send.at[0], text_part(3), [])
        far_part.start()

    @pl.when(core == 0)
    def _():
        core_send[1] = text_part(2)
        core_copy(1).start()

    text_sums(0)

    for way in (0, 1):
        block = image_part(tower_at(1 + 2 * way))
        kept[way] = block[way * half : (way + 1) * half]
        direct = block[(1 - way) * half : (2 - way) * half]
        put_rows(tower_send.at[way, pl.ds((1 - way) * half, half)], direct, loss_fields(total))
        block_copy(0, way, 0).start()

    own_image[...] = image_part(tower)

    order = order_ref
    loads[2].wait()
    place = lax.broadcasted_iota(jnp.int32, (quarter, quarter), 0)
    goal = lax.rem(z + z_step(lax.rem(place, n_z)), n_z) * PLANE + place // n_z
    picks = goal == order[...] // (n_tower * quarter)
    slots = jnp.sum(jnp.where(picks, lax.rem(order[...], quarter), 0), axis=1, keepdims=True)
    one_hot = jnp.where(picks, 1.0, 0.0).astype(jnp.bfloat16)

    count = mask_ref[0, 0] * 0
    for p in range(mask_ref.shape[0]):
        for c in range(mask_ref.shape[1]):
            count = count + mask_ref[p, c]

    def plane_copy(part, peer):
        first, last = ROW_PARTS[part]
        return remote(
            row_send.at[pl.ds(first, last - first), peer],
            row_mid.at[pl.ds(first, last - first), j],
            plane_sent,
            plane_here.at[part],
            {"batch": z * PLANE + peer},
        )

    def column_copy(part, i):
        first, last = ROW_PARTS[part]
        here = row_mid.at[pl.ds(first, last - first), :, pl.ds(i, 1), :]
        there = row_recv.at[pl.ds(first, last - first), :, pl.ds(i, 1), :]
        return remote(here, there, row_sent, row_here, {"batch": column_at(i)})

    def to_plane(part):
        first, last = ROW_PARTS[part]

        def some(i, _):
            plane_copy(part, lax.rem(j + i, PLANE)).start()
            return 0

        lax.fori_loop(1, PLANE, some, 0)
        for n in range(first, last):
            row_mid[n, pl.ds(j, 1)] = row_send[n, pl.ds(j, 1)]

    def to_column(part):
        first, last = ROW_PARTS[part]
        others = row_mid.at[pl.ds(first, last - first), pl.ds(0, PLANE - 1)]
        pltpu.make_async_copy(others, others, plane_here.at[part]).wait()

        def some(i, _):
            column_copy(part, i).start()
            return 0

        lax.fori_loop(0, n_z - 1, some, 0)

    def pass_on():
        for way in (0, 1):
            hop_copy(way).wait_recv()
            extras = low_of(hop_recv[way, 0:8, 0:LANES])
            both = total + loss_from(extras[0:1, 1:2], extras[0:1, 2:3], extras[0:1, 3:4])
            rows = kept[way] + get_rows(hop_recv.at[way])
            put_rows(tower_send.at[way, pl.ds(way * half, half)], rows, loss_fields(both))
            block_copy(0, way, 1).start()

    powers = []
    steps = []
    spare = None
    for part, (first, last) in enumerate(SUM_PARTS):
        if part == 0:
            pass_on()
        for way in (0, 1):
            for summed in (0, 1):
                block_copy(part, way, summed).wait_recv()
        if part == 0:
            for n in range(2):
                extras = low_of(tower_recv[n, :, 0:LANES])
                steps.append(step_of(extras[:, 0:1]))
                total = total + loss_from(extras[0:1, 1:2], extras[0:1, 2:3], extras[0:1, 3:4])
            spare = own_image[:, 8 * LANES :]
            for n in range(2):
                spare = spare + high_of(tower_recv[n, :, 0:LANES]).astype(jnp.float32) * steps[n]
        if part + 1 < len(SUM_PARTS):
            for way in (0, 1):
                block_copy(part + 1, way, 0).start()
                block_copy(part + 1, way, 1).start()
        rows = []
        for group in range(max(first, 1), last):
            high = own_image[:, (group - 1) * LANES : group * LANES]
            low = own_image[:, (group + 3) * LANES : (group + 4) * LANES]
            for n in range(2):
                word = tower_recv[n, :, group * LANES : (group + 1) * LANES]
                high = high + high_of(word).astype(jnp.float32) * steps[n]
                low = low + low_of(word).astype(jnp.float32) * steps[n]
            rows += [high, low]
        final = part == len(SUM_PARTS) - 1
        if final:
            rows.append(spare)
        codes, power = as_codes(jnp.concatenate(rows, axis=1))
        powers.append(power)
        if final:
            codes = jnp.concatenate([codes, fields(powers, quarter)], axis=1)
        codes = moved(one_hot, codes, NN).astype(jnp.int32)
        groups = [codes[:, LANES * n : LANES * (n + 1)] for n in range(codes.shape[1] // LANES)]
        if final:
            for n, value in enumerate([slots, count, *loss_fields(total)]):
                groups[-1] = jnp.where(lane_ids(quarter) == len(powers) + n, value, groups[-1])
        for n in range(len(groups) // 2):
            word = word_of(groups[2 * n], groups[2 * n + 1])
            row_send[ROW_PARTS[part][0] + n] = word.reshape(PLANE, n_z, LANES)
        to_plane(part)
        if part == 0:
            text_sums(1)
        to_column(part)

    own_here = row_mid.at[:, :, pl.ds(n_z - 1, 1), :]
    own_there = row_recv.at[:, :, pl.ds(n_z - 1, 1), :]
    own_copy = pltpu.make_async_copy(own_here, own_there, row_own)
    own_copy.start()

    near_part.wait_recv()
    own_text[...] += get_rows(part_recv.at[1])

    @pl.when(core == 1)
    def _():
        core_copy(0).wait_recv()
        own_text[...] += core_recv[0]

    back = own_text[...]
    wide = texts_ref[...].astype(jnp.float32)
    inv = row_inv(wide)
    unit = wide * inv
    text_grad_ref[...] = (back - unit * jnp.sum(unit * back, axis=-1, keepdims=True)) * inv
    text_out = pltpu.make_async_copy(text_grad_ref, text_hbm, out_here.at[0])
    text_out.start()

    own_copy.wait()
    all_rows = row_recv.at[:, :, pl.ds(0, n_z - 1), :]
    pltpu.make_async_copy(all_rows, all_rows, row_here).wait()
    words_out = pltpu.make_async_copy(row_recv, words_hbm, out_here.at[1])
    words_out.start()
    extras = low_of(row_recv[4]).reshape(quarter, LANES)
    n_powers = len(ROW_PARTS)
    tail = [extras[:, n_powers + n : n_powers + n + 1] for n in range(1, 5)]
    losses = jnp.sum(loss_from(*tail[1:]), axis=0, keepdims=True)
    counts = jnp.sum(tail[0].astype(jnp.float32), axis=0, keepdims=True)
    loss_ref[...] = losses / (counts * float(4 * quarter * quarter))

    for n in range(PIECES):
        outward(n).wait_send()
        pass_near(n).wait_send()

    @pl.when(core == 0)
    def _():
        for n in range(PIECES):
            to_relay(n).wait_send()
            pass_far(n).wait_send()
        core_copy(0).wait_send()

    @pl.when(core == 1)
    def _():
        for n in range(PIECES):
            to_sibling(n).wait_send()
        far_part.wait_send()

    core_copy(1).wait_send()
    near_part.wait_send()
    for way in (0, 1):
        hop_copy(way).wait_send()
        for part in range(len(SUM_PARTS)):
            for summed in (0, 1):
                block_copy(part, way, summed).wait_send()
    all_sent = row_send.at[:, pl.ds(0, PLANE - 1)]
    pltpu.make_async_copy(all_sent, all_sent, plane_sent).wait()
    pltpu.make_async_copy(all_rows, all_rows, row_sent).wait()
    text_out.wait()
    words_out.wait()


def hand_out(words_hbm, text_in, image_out, text_out, words_ref, text_ref, image_ref, done):
    words_in = pltpu.make_async_copy(words_hbm, words_ref, done.at[0])
    text_load = pltpu.make_async_copy(text_in, text_ref, done.at[1])
    image_store = pltpu.make_async_copy(image_ref, image_out, done.at[2])
    text_store = pltpu.make_async_copy(text_ref, text_out, done.at[3])
    words_in.start()
    text_load.start()
    words_in.wait()
    quarter = image_ref.shape[0]
    words = [words_ref[n].reshape(quarter, LANES) for n in range(5)]
    extras = low_of(words[4])
    n_powers = len(ROW_PARTS)
    places = jnp.where(lane_ids(quarter) == extras[:, n_powers : n_powers + 1], 1.0, 0.0)
    places = places.astype(jnp.bfloat16)
    sizes = jnp.exp(moved(places, extras, TN) * LOG_STEP) * (1.0 / TOP)
    text_load.wait()
    text_store.start()

    def put_group(group, whole, part):
        image_ref[:, LANES * group : LANES * (group + 1)] = (
            moved(places, whole, TN) * sizes[:, part : part + 1]
        )

    for part, (first, last) in enumerate(ROW_PARTS):
        for n in range(first, min(last, 4)):
            put_group(n, high_of(words[n]), part)
            put_group(n + 4, low_of(words[n]), part)
    put_group(8, high_of(words[4]), len(ROW_PARTS) - 1)
    image_store.start()
    text_store.wait()
    image_store.wait()


def shards(images, texts, log_scale, bias, block_mask, data_order):
    rows_group, width = images.shape
    quarter = texts.shape[0]
    words = 5 * LANES
    n_z = quarter // PLANE
    parts = len(SUM_PARTS)
    vmem = pl.BlockSpec(memory_space=pltpu.VMEM)
    smem = pl.BlockSpec(memory_space=pltpu.SMEM)
    hbm = pl.BlockSpec(memory_space=pl.ANY)
    dma = pltpu.SemaphoreType.DMA
    arrived, text_grad, pair_loss = pl.pallas_call(
        kernel,
        out_shape=(
            jax.ShapeDtypeStruct((5, PLANE, n_z, LANES), jnp.int32),
            jax.ShapeDtypeStruct((quarter, width), jnp.float32),
            jax.ShapeDtypeStruct((1, 1), jnp.float32),
        ),
        in_specs=[hbm, hbm, smem, smem, smem, hbm],
        out_specs=(hbm, hbm, vmem),
        scratch_shapes=[
            pltpu.VMEM((rows_group, width), jnp.bfloat16),
            pltpu.VMEM((quarter, width), jnp.bfloat16),
            pltpu.VMEM((1, quarter), jnp.int32),
            pltpu.VMEM((rows_group, width), jnp.bfloat16),
            pltpu.VMEM((rows_group, 1), jnp.float32),
            pltpu.VMEM((5, quarter, width), jnp.bfloat16),
            pltpu.VMEM((rows_group, 4 * quarter), jnp.bfloat16),
            pltpu.VMEM((rows_group, quarter), jnp.float32),
            pltpu.VMEM((quarter, quarter), jnp.float32),
            pltpu.VMEM((quarter, width), jnp.float32),
            pltpu.VMEM((quarter, width), jnp.float32),
            pltpu.VMEM((2, quarter, width), jnp.float32),
            pltpu.VMEM((2, quarter, width), jnp.float32),
            pltpu.VMEM((2, quarter, words), jnp.int32),
            pltpu.VMEM((2, quarter, words), jnp.int32),
            pltpu.VMEM((2, quarter, words), jnp.int32),
            pltpu.VMEM((2, quarter, words), jnp.int32),
            pltpu.VMEM((quarter, words), jnp.int32),
            pltpu.VMEM((2, quarter // 2, words), jnp.int32),
            pltpu.VMEM((2, quarter // 2, width), jnp.float32),
            pltpu.VMEM((5, PLANE, n_z, LANES), jnp.int32),
            pltpu.VMEM((5, PLANE, n_z, LANES), jnp.int32),
            pltpu.VMEM((5, PLANE, n_z, LANES), jnp.int32),
            dma((3,)),
            dma((4, PIECES)),
            dma((5, PIECES)),
            dma((2,)),
            dma((2,)),
            dma((2,)),
            dma((2,)),
            dma((2,)),
            dma((2,)),
            dma((parts, 2, 2)),
            dma((parts, 2, 2)),
            dma,
            dma((parts,)),
            dma,
            dma,
            dma,
            pltpu.VMEM((quarter, width), jnp.float32),
            dma((2,)),
        ],
        compiler_params=pltpu.CompilerParams(
            collective_id=0, has_side_effects=True, vmem_limit_bytes=64 * 1024 * 1024
        ),
    )(
        images,
        texts,
        log_scale.reshape(1),
        bias.reshape(1),
        block_mask,
        data_order.reshape(1, quarter),
    )
    image_grad, text_grad = pl.pallas_call(
        hand_out,
        out_shape=(
            jax.ShapeDtypeStruct((quarter, width), jnp.float32),
            jax.ShapeDtypeStruct((quarter, width), jnp.float32),
        ),
        in_specs=[pl.BlockSpec(memory_space=pltpu.HBM)] * 2,
        out_specs=(pl.BlockSpec(memory_space=pltpu.HBM),) * 2,
        scratch_shapes=[
            pltpu.VMEM((5, PLANE, n_z, LANES), jnp.int32),
            pltpu.VMEM((quarter, width), jnp.float32),
            pltpu.VMEM((quarter, width), jnp.float32),
            dma((4,)),
        ],
        compiler_params=pltpu.CompilerParams(vmem_limit_bytes=64 * 1024 * 1024),
    )(arrived, text_grad)
    return image_grad, text_grad, pair_loss.reshape(())


def solution(mesh):
    in_specs = (
        P("batch", None),
        P(("batch", "tower"), None),
        P(),
        P(),
        P("batch", None),
        P(("batch", "tower")),
    )
    out_specs = (P(("batch", "tower"), None), P(("batch", "tower"), None), P())
    return jax.shard_map(shards, mesh=mesh, in_specs=in_specs, out_specs=out_specs, check_vma=False)
```
